256 devices in a mesh: seq: 64 (over z, x, core), head: 4 (over y).
Axes of the slice: x: 4, y: 4, z: 8, core: 2. Of those that a mesh axis runs over, the one named last changes fastest.
Arguments:
- tokens: bfloat16 [32768, 1024], P('seq'), may hold values from -40 to 40
- query_weight: bfloat16 [1024, 1024], P(None, 'head'), may hold values from -0.1875 to 0.1875
- key_weight: bfloat16 [1024, 1024], P(None, 'head'), may hold values from -0.1875 to 0.1875
- value_weight: bfloat16 [1024, 1024], P(None, 'head'), may hold values from -0.1875 to 0.1875
- out_weight: bfloat16 [1024, 1024], P('head'), may hold values from -0.1875 to 0.1875
- level_gate: int32 [256, 16], P('seq'), may hold values 0 or 1
Outputs:
- mixed: bfloat16 [32768, 1024], P('seq', 'head')
The draws below stay inside these ranges and needn't reach their ends.
All inputs are finite; a program needn't handle non-finite values. No bound on the sum of `level_gate` on one device may be relied on, other than what follows from the above.
Results may differ from the reference program's by a relative error of at most 0.012.
The reference program's roundings to bfloat16 on the way (of `weights` and `attended`) count: a program that leaves them out, or rounds other values in their place, can miss the bound.
Values may be sent and summed in bfloat16 or wider, within the bound.
No kernel may reach another device: no remote copies, remote signals or barrier semaphores. Data moves between devices by JAX's collectives and lax.ppermute only.
A program may use at most 128 MiB of HBM per device.

```python
import math
import jax
import jax.numpy as jnp
from jax import lax

D = 1024
HEADS = 16
HEAD_DIM = 64
BLOCK = 128
GATE_COLS = 16
TOKENS = 32768
NBLOCKS = 256


def draw_tokens(key, part):
    key = jax.random.fold_in(key, 7)
    total = jax.random.normal(jax.random.fold_in(key, 1), (TOKENS, D), jnp.float32)
    levels = NBLOCKS.bit_length() - 1
    for level in range(levels):
        span = BLOCK << level
        coarse = jax.random.normal(jax.random.fold_in(key, 100 + level), (TOKENS // span, 1, D), jnp.float32)
        total = total + 0.5 * jnp.broadcast_to(coarse, (TOKENS // span, span, D)).reshape(TOKENS, D)
    return jnp.clip(total, -40.0, 40.0).astype(jnp.bfloat16)


def touch_ends(drawn, rng, smallest, top_value):
    longest = drawn.shape.index(max(drawn.shape))
    spots = []
    for shift in (0, 1):
        where = [jax.random.randint(jax.random.fold_in(rng, axis), (), 0, length) for axis, length in enumerate(drawn.shape)]
        where[longest] = (where[longest] + shift) % drawn.shape[longest]
        spots.append(tuple(where))
    return drawn.at[spots[0]].set(smallest).at[spots[1]].set(top_value)


def shard_levels(rng, dims, cuts, smallest, high):
    gain = 1.0
    for dim, parts in cuts:
        steps = jax.random.uniform(jax.random.fold_in(jax.random.fold_in(rng, 6), dim), (parts,), jnp.float32, smallest / len(cuts), high / len(cuts))
        gain = gain * jnp.repeat(jnp.exp(steps), dims[dim] // parts).reshape((-1,) + (1,) * (len(dims) - 1 - dim))
    return gain


def normal_values(own_key, dims, deviation, reach, cuts=(), held_as=jnp.bfloat16):
    entries = deviation * jax.random.normal(own_key, dims, jnp.float32)
    if cuts:
        entries = entries * shard_levels(own_key, dims, cuts, -0.22, 0.18)
    return jnp.clip(entries, -reach, reach).astype(held_as)


def setup_inputs(seed: int = 0) -> dict:
    splits = jax.random.split(jax.random.key(seed), 7)
    return {
        "tokens": draw_tokens(jax.random.fold_in(splits[6], 71), 0),
        "query_weight": normal_values(splits[1], (D, D), D ** -0.5, 0.1875, ((1, 4),)),
        "key_weight": normal_values(splits[2], (D, D), D ** -0.5, 0.1875, ((1, 4),)),
        "value_weight": normal_values(splits[3], (D, D), D ** -0.5, 0.1875, ((1, 4),)),
        "out_weight": normal_values(splits[4], (D, D), D ** -0.5, 0.1875, ((0, 4),)),
        "level_gate": touch_ends((jax.random.randint(splits[5], (NBLOCKS, GATE_COLS), 0, 4) < 3).astype(jnp.int32), jax.random.fold_in(splits[5], 1), 0, 1),
    }


LOG_TWO = math.log(2.0)
NEG_FILL = -1e30


def pool(array, level):
    count = array.shape[0] >> level
    shaped = array.reshape(count, 1 << level, array.shape[1])
    return jnp.mean(shaped, axis=1, dtype=jnp.float32).astype(jnp.bfloat16)


def reference(tokens, query_weight, key_weight, value_weight, out_weight, level_gate):
    query = jnp.dot(tokens, query_weight, preferred_element_type=jnp.float32).astype(jnp.bfloat16)
    keys = jnp.dot(tokens, key_weight, preferred_element_type=jnp.float32).astype(jnp.bfloat16)
    values = jnp.dot(tokens, value_weight, preferred_element_type=jnp.float32).astype(jnp.bfloat16)
    levels = NBLOCKS.bit_length() - 1
    key_levels = [pool(keys, level).reshape(-1, BLOCK, D) for level in range(levels)]
    value_levels = [pool(values, level).reshape(-1, BLOCK, D) for level in range(levels)]
    positions = jnp.arange(BLOCK, dtype=jnp.int32)
    causal = jnp.where(positions[None, :] <= positions[:, None], 0.0, NEG_FILL).astype(jnp.float32)

    def one_block(index):
        rows = lax.dynamic_slice_in_dim(query, index * BLOCK, BLOCK, 0)
        key_list = [lax.dynamic_slice_in_dim(keys, index * BLOCK, BLOCK, 0)]
        value_list = [lax.dynamic_slice_in_dim(values, index * BLOCK, BLOCK, 0)]
        bias_list = [causal]
        for level in range(levels):
            segment = index >> level
            sibling = jnp.maximum(segment - 1, 0).astype(jnp.int32)
            key_list.append(lax.dynamic_index_in_dim(key_levels[level], sibling, 0, keepdims=False))
            value_list.append(lax.dynamic_index_in_dim(value_levels[level], sibling, 0, keepdims=False))
            live = jnp.logical_and((segment & 1) == 1, level_gate[index, level] == 1)
            fill = jnp.where(live, level * LOG_TWO, NEG_FILL).astype(jnp.float32)
            bias_list.append(jnp.broadcast_to(fill, (BLOCK, BLOCK)))
        key_all = jnp.concatenate(key_list, axis=0).reshape(-1, HEADS, HEAD_DIM).astype(jnp.float32)
        value_all = jnp.concatenate(value_list, axis=0).reshape(-1, HEADS, HEAD_DIM).astype(jnp.float32)
        bias = jnp.concatenate(bias_list, axis=1)
        heads_q = rows.reshape(BLOCK, HEADS, HEAD_DIM).astype(jnp.float32)
        scores = jnp.einsum("qhd,khd->hqk", heads_q, key_all) * 0.125 + bias[None]
        top = jnp.max(scores, axis=-1, keepdims=True)
        expo = jnp.exp(scores - top)
        total = jnp.sum(expo, axis=-1, keepdims=True)
        weights = (expo / total).astype(jnp.bfloat16)
        result = jnp.einsum("hqk,khd->qhd", weights.astype(jnp.float32), value_all)
        return result.reshape(BLOCK, D).astype(jnp.bfloat16)

    attended = lax.map(one_block, jnp.arange(NBLOCKS, dtype=jnp.int32)).reshape(TOKENS, D)
    return jnp.dot(attended, out_weight, preferred_element_type=jnp.float32).astype(jnp.bfloat16)
```

```python
import functools
import math

import jax
import jax.numpy as jnp
from jax import lax
from jax.experimental import pallas as pl
from jax.experimental.pallas import tpu as pltpu
from jax.sharding import PartitionSpec as P

LOG_TWO = math.log(2.0)
NEG = -1e30
BLOCK = 128
WIDTH = 256
HEADS = 4
F32 = jnp.float32
BF16 = jnp.bfloat16

Z, X, C = 8, 4, 2


def index(z, x, c):
    return (z % Z) * 8 + (x % X) * 2 + c


CHIPS = [(z, x, c) for z in range(Z) for x in range(X) for c in range(C)]


def dot(a, b):
    return lax.dot_general(a, b, (((1,), (0,)), ((), ())), preferred_element_type=F32)


def pool_rows(rows, level):
    token = lax.broadcasted_iota(jnp.int32, (rows, 512), 1)
    row = lax.broadcasted_iota(jnp.int32, (rows, 512), 0)
    inverse = jnp.float32(0.0)
    for each in range(1, 8):
        inverse = jnp.where(level == each, jnp.float32(2.0**-each), inverse)
    hit = lax.shift_right_logical(token, jnp.full((rows, 512), level, jnp.int32)) == row
    return jnp.where(hit, inverse, 0.0).astype(BF16)


def blocks_kernel(tok, mean):
    mean[...] = jnp.zeros(mean.shape, F32)
    for b in range(4):
        part = tok[b * BLOCK : (b + 1) * BLOCK, :].astype(F32)
        mean[b : b + 1, :] = jnp.sum(part, axis=0, keepdims=True) * (1.0 / BLOCK)


def keys_kernel(tok, wk, wv, kv, l1, s0, e1, z3, z4):
    keys = dot(tok[...], wk[...]).astype(BF16)
    values = dot(tok[...], wv[...]).astype(BF16)
    both = jnp.concatenate([keys, values], axis=1)
    kv[...] = both
    parts = [pool_rows(n, level) for n, level in ((128, 2), (128, 1), (64, 3), (32, 4), (16, 5), (16, 6))]
    pooled = dot(jnp.concatenate(parts, axis=0), both)
    s0[...] = pooled[0:128].astype(BF16)
    l1[...] = pooled[128:256].astype(BF16)
    e1[...] = pooled[256:352].astype(BF16)
    z3[...] = pooled[352:368].astype(BF16)
    z4[...] = pooled[368:384].astype(BF16)


def far_rows_kernel(mean, wk, wv, z4, out):
    high = mean[...].astype(BF16)
    low = (mean[...] - high.astype(F32)).astype(BF16)
    both = jnp.concatenate([high.astype(F32), low.astype(F32)], axis=0).astype(BF16)
    for w, cols in ((wk, slice(0, WIDTH)), (wv, slice(WIDTH, 2 * WIDTH))):
        rows = dot(both, w[...])
        own = z4[:, cols].astype(F32)
        out[:, cols] = jnp.concatenate([own[:8], rows[:8] + rows[8:]], axis=0).astype(BF16)


def joint_kernel(z3, sent, got, out):
    sent, got = sent[...].astype(F32), got[...].astype(F32)
    last = jnp.concatenate([got[:8], sent[8:12], got[8:12]], axis=0).astype(BF16)
    out[0:16, :] = z3[...]
    out[16:32, :] = last


def far_join_kernel(sent, got, out):
    mine, other = sent[16:32, :].astype(F32), got[16:32, :].astype(F32)
    out[0:16, :] = got[0:16, :]
    out[16:32, :] = jnp.concatenate([mine[:8], other[:8]], axis=0).astype(BF16)
    out[32:48, :] = jnp.concatenate([mine[8:], other[8:]], axis=0).astype(BF16)


def near_join_kernel(sent, got, out):
    out[0:32, :] = sent[64:96, :]
    out[32:64, :] = got[64:96, :]


def plane_join_kernel(s0, first, second, out):
    out[0:128, :] = s0[...]
    out[128:192, :] = first[0:64, :]
    out[192:256, :] = second[...]


def row_join_kernel(a, b, c, d, out):
    for step, piece in enumerate((a, b, c, d)):
        out[step * 48 : (step + 1) * 48, :] = piece[...]


def stack_heads(query_t):
    head = lax.broadcasted_iota(jnp.int32, (WIDTH, BLOCK), 0) // 64
    zero = jnp.zeros_like(query_t)
    return jnp.concatenate([jnp.where(head == h, query_t, zero) for h in range(HEADS)], axis=1)


def pick_heads(stacked):
    return jnp.concatenate(
        [stacked[h * 64 : (h + 1) * 64, h * BLOCK : (h + 1) * BLOCK] for h in range(HEADS)], axis=0
    )


def spread_heads(row):
    return jnp.concatenate(
        [jnp.broadcast_to(row[:, h * BLOCK : (h + 1) * BLOCK], (64, BLOCK)) for h in range(HEADS)],
        axis=0,
    )


def turn(array):
    return array.astype(F32).T.astype(BF16)


def gate_bias(gate, block, level):
    return jnp.where(gate[block, level] == 1, jnp.float32(level * LOG_TWO), jnp.float32(NEG))


def four(array):
    return jnp.concatenate([array] * 4, axis=1)


def own_kernel(gate, tok, wq, kv, l1, qt, acc, ml):
    query = dot(tok[...], wq[...]).astype(BF16).astype(F32) * 0.125
    query_t = query.T.astype(BF16)
    qt[...] = query_t
    key = lax.broadcasted_iota(jnp.int32, (BLOCK, BLOCK), 0)
    row = lax.broadcasted_iota(jnp.int32, (BLOCK, BLOCK), 1)
    causal = jnp.where(key <= row, 0.0, NEG).astype(F32)
    values_t = turn(kv[:, WIDTH:])
    l1_t = turn(l1[:, WIDTH:])
    for b in range(4):
        rows = slice(b * BLOCK, (b + 1) * BLOCK)
        keys = [kv[rows, :WIDTH]]
        values = [values_t[:, rows]]
        bias = [causal]
        if b & 1:
            before = slice((b - 1) * BLOCK, b * BLOCK)
            keys.append(kv[before, :WIDTH])
            values.append(values_t[:, before])
            bias.append(jnp.full((BLOCK, BLOCK), gate_bias(gate, b, 0)))
        if b & 2:
            keys.append(l1[:, :WIDTH])
            values.append(l1_t)
            bias.append(jnp.full((BLOCK, BLOCK), gate_bias(gate, b, 1)))
        scores = dot(jnp.concatenate(keys, axis=0), stack_heads(query_t[:, rows]))
        scores = scores + four(jnp.concatenate(bias, axis=0))
        top = jnp.max(scores, axis=0, keepdims=True)
        expo = jnp.exp(scores - top)
        ml[b : b + 1, :] = top
        ml[4 + b : 5 + b, :] = jnp.sum(expo, axis=0, keepdims=True)
        acc[:, rows] = pick_heads(dot(jnp.concatenate(values, axis=1), expo.astype(BF16)))


def plane_levels():
    seq = lax.axis_index("seq")
    have = [jnp.where(lax.shift_right_logical(seq, bit) % 2 == 1, 2 + bit, -1) for bit in range(3)]
    spot = lax.broadcasted_iota(jnp.int32, (384, BLOCK), 0)
    return jnp.where(spot < 128, have[0], jnp.where(spot % 128 < 64, have[1], have[2]))


def far_levels():
    z = lax.axis_index("seq") // 8
    spot = lax.broadcasted_iota(jnp.int32, (384, BLOCK), 0) % 48
    have = [jnp.where(lax.shift_right_logical(z, bit) % 2 == 1, 5 + bit, -1) for bit in range(3)]
    return jnp.where(spot < 16, have[0], jnp.where(spot < 32, have[1], have[2]))


def bias_rows(gate, block, levels, used):
    bias = jnp.full(levels.shape, NEG, F32)
    for level in used:
        bias = jnp.where(levels == level, gate_bias(gate, block, level), bias)
    return four(bias)


def cross(b, qt, acc, ml, keys, values_t, bias):
    rows = slice(b * BLOCK, (b + 1) * BLOCK)
    old_top, old_total = ml[b : b + 1, :], ml[4 + b : 5 + b, :]
    scores = dot(keys, stack_heads(qt[:, rows])) + bias
    top = jnp.maximum(old_top, jnp.max(scores, axis=0, keepdims=True))
    expo = jnp.exp(scores - top)
    scale = jnp.exp(old_top - top)
    total = old_total * scale + jnp.sum(expo, axis=0, keepdims=True)
    out = pick_heads(dot(values_t, expo.astype(BF16)))
    return acc[:, rows] * spread_heads(scale) + out, top, total


def plane_kernel(gate, qt, acc, ml, first, second, other, acc_out, ml_out):
    pieces = [other[0:128, :], first[0:64, :], second[...], other[128:256, :]]
    keys = jnp.concatenate([piece[:, :WIDTH] for piece in pieces], axis=0)
    values_t = turn(jnp.concatenate([piece[:, WIDTH:] for piece in pieces], axis=0))
    levels = plane_levels()
    for b in range(4):
        bias = bias_rows(gate, b, levels, (2, 3, 4))
        out, top, total = cross(b, qt, acc, ml, keys, values_t, bias)
        acc_out[:, b * BLOCK : (b + 1) * BLOCK] = out
        ml_out[b : b + 1, :] = top
        ml_out[4 + b : 5 + b, :] = total


def far_kernel(half, gate, qt, acc, ml, mine, other, att):
    keys = jnp.concatenate([mine[:, :WIDTH], other[:, :WIDTH]], axis=0)
    values_t = turn(jnp.concatenate([mine[:, WIDTH:], other[:, WIDTH:]], axis=0))
    levels = far_levels()
    for step in range(2):
        b = half * 2 + step
        bias = bias_rows(gate, b, levels, (5, 6, 7))
        out, _, total = cross(b, qt, acc, ml, keys, values_t, bias)
        att[step * BLOCK : (step + 1) * BLOCK, :] = (out / spread_heads(total)).T.astype(BF16)


def project_kernel(half, mine_att, peer_att, mine_w, peer_w, keep, send):
    head = lax.axis_index("head")
    other = (3 - head) if half == 0 else (head + 1 - 2 * (head % 2))
    for where, ref in ((other, send), (head, keep)):
        cols = pl.ds(pl.multiple_of(where * WIDTH, WIDTH), WIDTH)
        total = dot(mine_att[...], mine_w[:, cols]) + dot(peer_att[...], peer_w[:, cols])
        ref[...] = total.astype(ref.dtype)


VMEM = pl.BlockSpec(memory_space=pltpu.VMEM)
SMEM = pl.BlockSpec(memory_space=pltpu.SMEM)


def call(kernel, args, outs, flops, smem=0):
    return pl.pallas_call(
        kernel,
        out_shape=[jax.ShapeDtypeStruct(shape, dtype) for shape, dtype in outs],
        in_specs=[SMEM] * smem + [VMEM] * (len(args) - smem),
        out_specs=[VMEM] * len(outs),
        compiler_params=pltpu.CompilerParams(vmem_limit_bytes=24 * 1024 * 1024),
        cost_estimate=pl.CostEstimate(flops=flops, bytes_accessed=1000, transcendentals=0),
    )(*args)


def move(array, pairs):
    return lax.ppermute(array, "seq", pairs)


def plane(array, to):
    return move(array, [(index(z, x, c), index(to(z), x, c)) for z, x, c in CHIPS])


def along(array, shift):
    return move(array, [(index(z, x, c), index(z, x + shift, c)) for z, x, c in CHIPS])


def across(array, bit):
    return move(array, [(index(z, x, c), index(z, x ^ bit, c)) for z, x, c in CHIPS])


def swap(array):
    return move(array, [(index(z, x, c), index(z, x, 1 - c)) for z, x, c in CHIPS])


PAIR_NEXT = [(0, 1), (1, 0), (2, 3), (3, 2)]
PAIR_FAR = [(0, 3), (3, 0), (1, 2), (2, 1)]


def shards(tokens, wq, wk, wv, wo, gate):
    rows = lambda n: ((n, 2 * WIDTH), BF16)
    (mean,) = call(blocks_kernel, (tokens,), [((8, 1024), F32)], 2 * 10**8)
    mean_up = plane(mean, lambda z: 7 - z)
    kv, l1, s0, e1, z3, z4 = call(
        keys_kernel,
        (tokens, wk, wv),
        [rows(512), rows(128), rows(128), rows(96), rows(16), rows(16)],
        10**9,
    )
    wo_next = lax.ppermute(wo, "head", PAIR_NEXT)
    wo_far = lax.ppermute(wo, "head", PAIR_FAR)
    first = across(e1, 1)
    (pay,) = call(near_join_kernel, (e1, first), [rows(64)], 10**8)
    second = across(pay, 2)
    (pay,) = call(plane_join_kernel, (s0, first, second), [rows(256)], 10**8)
    other = swap(pay)
    qt, acc, ml = call(
        own_kernel,
        (gate, tokens, wq, kv, l1),
        [((WIDTH, 512), BF16), ((WIDTH, 512), F32), ((8, 512), F32)],
        3 * 10**9,
        smem=1,
    )
    (pay,) = call(far_rows_kernel, (mean_up, wk, wv, z4), [rows(16)], 2 * 10**8)
    got = plane(pay, lambda z: z ^ 2)
    (pay,) = call(joint_kernel, (z3, pay, got), [rows(32)], 10**8)
    got = plane(pay, lambda z: z ^ 1)
    (far,) = call(far_join_kernel, (pay, got), [rows(48)], 10**8)
    others = [along(far, shift) for shift in (1, -1, 2)]
    (far,) = call(row_join_kernel, (far, *others), [rows(192)], 10**8)
    far_other = swap(far)
    acc, ml = call(
        plane_kernel,
        (gate, qt, acc, ml, first, second, other),
        [((WIDTH, 512), F32), ((8, 512), F32)],
        3 * 10**9,
        smem=1,
    )
    halves = []
    for half in range(2):
        (att,) = call(
            functools.partial(far_kernel, half),
            (gate, qt, acc, ml, far, far_other),
            [((256, WIDTH), BF16)],
            2 * 10**9,
            smem=1,
        )
        halves.append(att)
    out = []
    pairs = (PAIR_NEXT, PAIR_FAR)
    for half in range(2):
        peer = lax.ppermute(halves[half], "head", pairs[half])
        keep, send = call(
            functools.partial(project_kernel, half),
            (halves[half], peer, wo, (wo_next, wo_far)[half]),
            [((256, WIDTH), F32), ((256, WIDTH), BF16)],
            10**8,
        )
        out.append(keep + lax.ppermute(send, "head", pairs[1 - half]).astype(F32))
    return jnp.concatenate(out, axis=0).astype(BF16)


def solution(mesh):
    placed = (
        P("seq", None),
        P(None, "head"),
        P(None, "head"),
        P(None, "head"),
        P("head", None),
        P("seq", None),
    )
    return jax.shard_map(
        shards, mesh=mesh, in_specs=placed, out_specs=P("seq", "head"), check_vma=False
    )
```

```python
import functools
import math

import jax
import jax.numpy as jnp
from jax import lax
from jax.experimental import pallas as pl
from jax.experimental.pallas import tpu as pltpu
from jax.sharding import PartitionSpec as P

LOG_TWO = math.log(2.0)
NEG = -1e30
BLOCK = 128
WIDTH = 256
HEADS = 4
F32 = jnp.float32
BF16 = jnp.bfloat16

Z, X, C = 8, 4, 2


def index(z, x, c):
    return (z % Z) * 8 + (x % X) * 2 + c


CHIPS = [(z, x, c) for z in range(Z) for x in range(X) for c in range(C)]


def dot(a, b):
    return lax.dot_general(a, b, (((1,), (0,)), ((), ())), preferred_element_type=F32)


def pool_rows(rows, level):
    token = lax.broadcasted_iota(jnp.int32, (rows, 512), 1)
    row = lax.broadcasted_iota(jnp.int32, (rows, 512), 0)
    inverse = jnp.float32(0.0)
    for each in range(1, 8):
        inverse = jnp.where(level == each, jnp.float32(2.0**-each), inverse)
    hit = lax.shift_right_logical(token, jnp.full((rows, 512), level, jnp.int32)) == row
    return jnp.where(hit, inverse, 0.0).astype(BF16)


def my_core():
    return lax.axis_index("seq") % 2


def load_kernel(
    tok_hbm, wk_hbm, wv_hbm, wo_hbm,
    kv, l1, e1, share, to_next, to_far,
    tok, wk, wv, sems,
):
    head = lax.axis_index("head")
    near, far = next_head(head), 3 - head
    pairs = [(wk_hbm, wk)]
    pairs += [(tok_hbm.at[pl.ds(i * 256, 256)], tok.at[pl.ds(i * 256, 256)]) for i in range(2)]
    pairs.append((wv_hbm, wv))
    for out, first, second in ((to_next, near, 3 - near), (to_far, far, next_head(far))):
        pairs.append((wo_hbm.at[:, columns(first)], out.at[:, pl.ds(0, WIDTH)]))
        pairs.append((wo_hbm.at[:, columns(second)], out.at[:, pl.ds(WIDTH, WIDTH)]))
    copies = [pltpu.make_async_copy(*pair, sems.at[i]) for i, pair in enumerate(pairs)]
    for copy in copies:
        copy.start()
    parts = [
        pool_rows(n, level)
        for n, level in ((128, 1), (64, 3), (32, 4), (128, 2), (16, 5), (16, 6), (16, 7))
    ]
    for copy in copies[:3]:
        copy.wait()
    keys = dot(tok[...], wk[...]).astype(BF16)
    copies[3].wait()
    values = dot(tok[...], wv[...]).astype(BF16)
    both = jnp.concatenate([keys, values], axis=1)
    kv[...] = both
    pooled = dot(jnp.concatenate(parts, axis=0), both)
    l1[...] = pooled[0:128].astype(BF16)
    e1[...] = pooled[128:224].astype(BF16)
    share[...] = pooled[224:400].astype(BF16)
    for copy in copies[4:]:
        copy.wait()


def mirror_kernel(share, other, after, out):
    own, far = share[160:176, :].astype(F32)[:4], other[160:176, :].astype(F32)[:4]
    out[...] = jnp.concatenate([own, far, own, far], axis=0).astype(BF16)


def two_kernel(share, other, got, after0, after1, out):
    own, far = share[144:160, :].astype(F32)[:8], other[144:160, :].astype(F32)[:8]
    out[0:16, :] = jnp.concatenate([own, far], axis=0).astype(BF16)
    out[16:32, :] = got[...]


def joint_kernel(share, other, sent, got, after, out):
    out[0:16, :] = share[128:144, :]
    out[16:32, :] = other[128:144, :]
    out[32:48, :] = got[0:16, :]
    mine, peer = sent[16:32, :].astype(F32)[:8], got[16:32, :].astype(F32)[:8]
    out[48:64, :] = jnp.concatenate([mine, peer], axis=0).astype(BF16)


def far_join_kernel(sent, got, out):
    out[0:32, :] = got[0:32, :]
    for level in (1, 2):
        to, at = level * 32, 16 + level * 16
        out[to : to + 16, :] = sent[at : at + 16, :]
        out[to + 16 : to + 32, :] = got[at : at + 16, :]


def near_join_kernel(sent, got, out):
    out[0:32, :] = sent[64:96, :]
    out[32:64, :] = got[64:96, :]


def plane_join_kernel(first, second, out):
    out[0:64, :] = first[0:64, :]
    out[64:128, :] = second[...]


def row_join_kernel(a, b, c, d, *refs):
    out = refs[-1]
    for level in range(3):
        for step, piece in enumerate((a, b, c, d)):
            to = level * 128 + step * 32
            out[to : to + 32, :] = piece[level * 32 : (level + 1) * 32, :]


def columns(chunk):
    return pl.ds(pl.multiple_of(chunk * WIDTH, WIDTH), WIDTH)


def next_head(head):
    return head + 1 - 2 * (head % 2)


def stack_heads(query_t):
    head = lax.broadcasted_iota(jnp.int32, (WIDTH, BLOCK), 0) // 64
    zero = jnp.zeros_like(query_t)
    return jnp.concatenate([jnp.where(head == h, query_t, zero) for h in range(HEADS)], axis=1)


def turn(array):
    return array.astype(F32).T.astype(BF16)


def gate_bias(gate, block, level):
    return jnp.where(gate[block, level] == 1, jnp.float32(level * LOG_TWO), jnp.float32(NEG))


def attend(query_t, keys, values_t, biases, mask, old, old_top, old_total):
    scores = dot(keys, stack_heads(query_t))
    outs, tops, totals = [], [], []
    for h in range(HEADS):
        lanes = slice(h * BLOCK, (h + 1) * BLOCK)
        pieces = [scores[i * BLOCK : (i + 1) * BLOCK, lanes] for i in range(len(biases))]
        if mask is not None:
            pieces[0] = pieces[0] + mask
        top = None if old_top is None else old_top[:, lanes]
        for piece, bias in zip(pieces, biases):
            high = jnp.max(piece, axis=0, keepdims=True) + bias
            top = high if top is None else jnp.maximum(top, high)
        expo = [jnp.exp(piece - (top - bias)) for piece, bias in zip(pieces, biases)]
        total = sum(jnp.sum(piece, axis=0, keepdims=True) for piece in expo)
        weights = jnp.concatenate([piece.astype(BF16) for piece in expo], axis=0)
        rows = slice(h * 64, (h + 1) * 64)
        out = dot(values_t[rows, :], weights)
        if old is not None:
            scale = jnp.exp(old_top[:, lanes] - top)
            out = out + old[rows, :] * scale
            total = total + old_total[:, lanes] * scale
        outs.append(out)
        tops.append(top)
        totals.append(total)
    return outs, tops, totals


def own_half(half, gate, qt, kv, vt, l1, acc, ml):
    key = lax.broadcasted_iota(jnp.int32, (BLOCK, BLOCK), 0)
    row = lax.broadcasted_iota(jnp.int32, (BLOCK, BLOCK), 1)
    causal = jnp.where(key <= row, 0.0, NEG).astype(F32)
    if half:
        l1_t = turn(l1[:, WIDTH:])
    for step in range(2):
        b = half * 2 + step
        rows = slice(b * BLOCK, (b + 1) * BLOCK)
        keys = [kv[rows, :WIDTH]]
        values = [vt[:, rows]]
        biases = [jnp.float32(0.0)]
        if b & 1:
            before = slice((b - 1) * BLOCK, b * BLOCK)
            keys.append(kv[before, :WIDTH])
            values.append(vt[:, before])
            biases.append(gate_bias(gate, b, 0))
        if b & 2:
            keys.append(l1[:, :WIDTH])
            values.append(l1_t)
            biases.append(gate_bias(gate, b, 1))
        keys, values = jnp.concatenate(keys, axis=0), jnp.concatenate(values, axis=1)
        outs, tops, totals = attend(qt[:, rows], keys, values, biases, causal, None, None, None)
        acc[:, step * BLOCK : (step + 1) * BLOCK] = jnp.concatenate(outs, axis=0)
        ml[step : step + 1, :] = jnp.concatenate(tops, axis=1)
        ml[4 + step : 5 + step, :] = jnp.concatenate(totals, axis=1)


def own_blocks(gate, tok, wq, kv, l1, qt, acc0, ml0, acc1, ml1):
    query = dot(tok[...], wq[...]).astype(BF16).astype(F32) * 0.125
    query_t = query.T.astype(BF16)
    qt[...] = query_t
    values_t = turn(kv[:, WIDTH:])
    own_half(0, gate, query_t, kv, values_t, l1, acc0, ml0)
    own_half(1, gate, query_t, kv, values_t, l1, acc1, ml1)


def high_plane():
    return lax.axis_index("seq") >= 32


def early_kernel(gate, tok, wq, kv, l1, *outs):
    @pl.when(jnp.logical_not(high_plane()))
    def _():
        own_blocks(gate, tok, wq, kv, l1, *outs)


def late_kernel(gate, tok, wq, kv, l1, *refs):
    early, outs = refs[:5], refs[-5:]

    @pl.when(high_plane())
    def _():
        own_blocks(gate, tok, wq, kv, l1, *outs)

    @pl.when(jnp.logical_not(high_plane()))
    def _():
        for source, out in zip(early, outs):
            out[...] = source[...]


def level_biases(gate, block, first):
    seq = lax.axis_index("seq")
    out = []
    for level in range(first, first + 3):
        bit = lax.shift_right_logical(seq, level - 2) % 2
        out.append(jnp.where(bit == 1, gate_bias(gate, block, level), jnp.float32(NEG)))
    return out


def cross(b, first, gate, qt, acc, ml, keys, values_t):
    step = b % 2
    biases = level_biases(gate, b, first)
    old = (acc[:, step * BLOCK : (step + 1) * BLOCK], ml[step : step + 1, :], ml[4 + step : 5 + step, :])
    return attend(qt[:, b * BLOCK : (b + 1) * BLOCK], keys, values_t, biases, None, *old)


def plane_kernel(gate, qt, acc0, ml0, acc1, ml1, share, first, second, other, *refs):
    outs_refs = refs[-4:]
    pieces = [share[0:128, :], first[0:64, :], other[0:64, :], second[...], other[64:128, :]]
    keys = jnp.concatenate([piece[:, :WIDTH] for piece in pieces], axis=0)
    values_t = turn(jnp.concatenate([piece[:, WIDTH:] for piece in pieces], axis=0))
    for b in range(4):
        half, step = b // 2, b % 2
        acc, ml = ((acc0, ml0), (acc1, ml1))[half]
        acc_out, ml_out = outs_refs[2 * half : 2 * half + 2]
        outs, tops, totals = cross(b, 2, gate, qt, acc, ml, keys, values_t)
        acc_out[:, step * BLOCK : (step + 1) * BLOCK] = jnp.concatenate(outs, axis=0)
        ml_out[step : step + 1, :] = jnp.concatenate(tops, axis=1)
        ml_out[4 + step : 5 + step, :] = jnp.concatenate(totals, axis=1)


def far_kernel(half, gate, qt, acc, ml, mine, other, att):
    rows = jnp.where(my_core() == 1, mine[...], other[...])
    keys = rows[:, :WIDTH]
    values_t = turn(rows[:, WIDTH:])
    for step in range(2):
        outs, _, totals = cross(half * 2 + step, 5, gate, qt, acc, ml, keys, values_t)
        outs = [out / total for out, total in zip(outs, totals)]
        turned = jnp.concatenate(outs, axis=0).T.astype(BF16)
        att[step * BLOCK : (step + 1) * BLOCK, :] = turned


def project_kernel(half, mine_att, peer_att, mine_w, peer_w, keep, send):
    head = lax.axis_index("head")
    other = 3 - head if half == 0 else next_head(head)
    for chunk, part, ref in ((other, slice(WIDTH, 2 * WIDTH), send), (head, slice(0, WIDTH), keep)):
        total = dot(mine_att[...], mine_w[:, columns(chunk)]) + dot(peer_att[...], peer_w[:, part])
        ref[...] = total.astype(ref.dtype)


VMEM = pl.BlockSpec(memory_space=pltpu.VMEM)
SMEM = pl.BlockSpec(memory_space=pltpu.SMEM)
ANY = pl.BlockSpec(memory_space=pl.ANY)
HBM = pl.BlockSpec(memory_space=pltpu.HBM)


def call(kernel, args, outs, flops, smem=0, unread=0):
    return pl.pallas_call(
        kernel,
        name=getattr(kernel, "func", kernel).__name__,
        out_shape=[jax.ShapeDtypeStruct(shape, dtype) for shape, dtype in outs],
        in_specs=[SMEM] * smem + [VMEM] * (len(args) - smem - unread) + [ANY] * unread,
        out_specs=[VMEM] * len(outs),
        compiler_params=pltpu.CompilerParams(vmem_limit_bytes=24 * 1024 * 1024),
        cost_estimate=pl.CostEstimate(flops=flops, bytes_accessed=1000, transcendentals=0),
    )(*args)


def move(array, pairs, name):
    with jax.named_scope(name):
        return lax.ppermute(array, "seq", pairs)


def hub(array, to, idle, name):
    far = [(index(z, x, 1), index(*to(z, x), 1)) for z, x, c in CHIPS if c]
    near = [(index(z, x, 0), index(*idle(z, x), 0)) for z, x, c in CHIPS if not c]
    return move(array, far + near, name)


def idle_x(z, x):
    return z, x ^ 1


def idle_z(z, x):
    return z ^ 1, x


def across(array, bit, name):
    return move(array, [(index(z, x, c), index(z, x ^ bit, c)) for z, x, c in CHIPS], name)


def swap(array, name):
    return move(array, [(index(z, x, c), index(z, x, 1 - c)) for z, x, c in CHIPS], name)


PAIR_NEXT = [(0, 1), (1, 0), (2, 3), (3, 2)]
PAIR_FAR = [(0, 3), (3, 0), (1, 2), (2, 1)]


COST = 10**6


def shards(tokens, wq, wk, wv, wo, gate):
    rows = lambda n: ((n, 2 * WIDTH), BF16)
    kv, l1, e1, share, to_next, to_far = pl.pallas_call(
        load_kernel,
        name="load_kernel",
        out_shape=[
            jax.ShapeDtypeStruct(shape, BF16)
            for shape in ((512, 512), (128, 512), (96, 512), (176, 512))
            + ((WIDTH, 512),) * 2
        ],
        in_specs=[HBM] * 4,
        out_specs=[VMEM] * 6,
        scratch_shapes=[
            pltpu.VMEM((512, 1024), BF16),
            pltpu.VMEM((1024, WIDTH), BF16),
            pltpu.VMEM((1024, WIDTH), BF16),
            pltpu.SemaphoreType.DMA((8,)),
        ],
        compiler_params=pltpu.CompilerParams(vmem_limit_bytes=52 * 1024 * 1024),
        cost_estimate=pl.CostEstimate(flops=COST, bytes_accessed=1000, transcendentals=0),
    )(tokens, wk, wv, wo)
    share_other = swap(share, "swap_share")
    first = across(e1, 1, "across_one")
    state = [((WIDTH, 256), F32), ((8, 512), F32)]
    held = [((WIDTH, 512), BF16)] + state * 2
    early = call(early_kernel, (gate, tokens, wq, kv, l1), held, COST, smem=1)
    (pay,) = call(mirror_kernel, (share, share_other, early[2]), [rows(16)], COST, unread=1)
    far5 = hub(pay, lambda z, x: (7 - z, x), idle_x, "planes_mirror")
    qt, acc0, ml0, acc1, ml1 = call(
        late_kernel, (gate, tokens, wq, kv, l1, *early, pay), held, COST, smem=1, unread=1
    )
    own = [(acc0, ml0), (acc1, ml1)]
    first, ml = lax.optimization_barrier((first, own[1][1]))
    own[1] = (own[1][0], ml)
    (near,) = call(near_join_kernel, (e1, first), [rows(64)], COST)
    second = across(near, 2, "across_two")
    (pay,) = call(
        two_kernel, (share, share_other, far5, own[0][1], own[1][1]), [rows(32)], COST, unread=2
    )
    got = hub(pay, lambda z, x: (z ^ 2, x), idle_x, "planes_two")
    (pay,) = call(
        joint_kernel, (share, share_other, pay, got, own[0][1]), [rows(64)], COST, unread=1
    )
    got = hub(pay, lambda z, x: (z ^ 1, x), idle_x, "planes_one")
    (far,) = call(far_join_kernel, (pay, got), [rows(96)], COST)
    (near,) = call(plane_join_kernel, (first, second), [rows(128)], COST)
    other = swap(near, "swap_near")
    far, to_far, to_next = lax.optimization_barrier((far, to_far, to_next))
    w_next = lax.ppermute(to_next, "head", PAIR_NEXT)
    w_far = lax.ppermute(to_far, "head", PAIR_FAR)
    acc0, ml0, acc1, ml1 = call(
        plane_kernel,
        (gate, qt, *own[0], *own[1], share_other, first, second, other),
        state * 2,
        COST,
        smem=1,
    )
    others = [hub(far, lambda z, x, shift=shift: (z, x + shift), idle_z, "along") for shift in (1, -1, 2)]
    (far,) = call(row_join_kernel, (far, *others, ml0, w_next, w_far), [rows(384)], COST, unread=3)
    far_other = swap(far, "swap_far")
    held = ((acc0, ml0), (acc1, ml1))
    halves = []
    for half in range(2):
        (att,) = call(
            functools.partial(far_kernel, half),
            (gate, qt, *held[half], far, far_other),
            [((256, WIDTH), BF16)],
            COST,
            smem=1,
        )
        halves.append(att)
    out = []
    pairs = (PAIR_NEXT, PAIR_FAR)
    for half in range(2):
        peer = lax.ppermute(halves[half], "head", pairs[half])
        keep, send = call(
            functools.partial(project_kernel, half),
            (halves[half], peer, wo, (w_next, w_far)[half]),
            [((256, WIDTH), F32), ((256, WIDTH), BF16)],
            COST,
        )
        out.append(keep + lax.ppermute(send, "head", pairs[1 - half]).astype(F32))
    return jnp.concatenate(out, axis=0).astype(BF16)


def solution(mesh):
    placed = (
        P("seq", None),
        P(None, "head"),
        P(None, "head"),
        P(None, "head"),
        P("head", None),
        P("seq", None),
    )
    return jax.shard_map(
        shards, mesh=mesh, in_specs=placed, out_specs=P("seq", "head"), check_vma=False
    )
```

```python
import functools
import math

import jax
import jax.numpy as jnp
from jax import lax
from jax.experimental import pallas as pl
from jax.experimental.pallas import tpu as pltpu
from jax.sharding import PartitionSpec as P

LOG_TWO = math.log(2.0)
NEG = -1e30
BLOCK = 128
WIDTH = 256
HEADS = 4
F32 = jnp.float32
BF16 = jnp.bfloat16

Z, X, C = 8, 4, 2


def index(z, x, c):
    return (z % Z) * 8 + (x % X) * 2 + c


CHIPS = [(z, x, c) for z in range(Z) for x in range(X) for c in range(C)]


def dot(a, b):
    return lax.dot_general(a, b, (((1,), (0,)), ((), ())), preferred_element_type=F32)


def pool_rows(rows, level):
    token = lax.broadcasted_iota(jnp.int32, (rows, 512), 1)
    row = lax.broadcasted_iota(jnp.int32, (rows, 512), 0)
    inverse = jnp.float32(0.0)
    for each in range(1, 8):
        inverse = jnp.where(level == each, jnp.float32(2.0**-each), inverse)
    hit = lax.shift_right_logical(token, jnp.full((rows, 512), level, jnp.int32)) == row
    return jnp.where(hit, inverse, 0.0).astype(BF16)


def my_core():
    return lax.axis_index("seq") % 2


def load_kernel(
    tok_hbm, wk_hbm, wv_hbm, wo_hbm,
    kv, l1, e1, share, to_next, to_far,
    tok, wk, wv, sems,
):
    head = lax.axis_index("head")
    near, far = next_head(head), 3 - head
    pairs = [(wk_hbm, wk)]
    pairs += [(tok_hbm.at[pl.ds(i * 256, 256)], tok.at[pl.ds(i * 256, 256)]) for i in range(2)]
    pairs.append((wv_hbm, wv))
    for out, first, second in ((to_next, near, 3 - near), (to_far, far, next_head(far))):
        pairs.append((wo_hbm.at[:, columns(first)], out.at[:, pl.ds(0, WIDTH)]))
        pairs.append((wo_hbm.at[:, columns(second)], out.at[:, pl.ds(WIDTH, WIDTH)]))
    copies = [pltpu.make_async_copy(*pair, sems.at[i]) for i, pair in enumerate(pairs)]
    for copy in copies:
        copy.start()
    parts = [
        pool_rows(n, level)
        for n, level in ((128, 1), (64, 3), (32, 4), (128, 2), (16, 5), (16, 6), (16, 7))
    ]
    for copy in copies[:3]:
        copy.wait()
    keys = dot(tok[...], wk[...]).astype(BF16)
    copies[3].wait()
    values = dot(tok[...], wv[...]).astype(BF16)
    both = jnp.concatenate([keys, values], axis=1)
    kv[...] = both
    pooled = dot(jnp.concatenate(parts, axis=0), both)
    l1[...] = pooled[0:128].astype(BF16)
    e1[...] = pooled[128:224].astype(BF16)
    share[...] = pooled[224:400].astype(BF16)
    for copy in copies[4:]:
        copy.wait()


def mirror_kernel(share, other, after, out):
    own, far = share[160:176, :].astype(F32)[:4], other[160:176, :].astype(F32)[:4]
    out[...] = jnp.concatenate([own, far, own, far], axis=0).astype(BF16)


def two_kernel(share, other, got, after0, after1, out):
    own, far = share[144:160, :].astype(F32)[:8], other[144:160, :].astype(F32)[:8]
    out[0:16, :] = jnp.concatenate([own, far], axis=0).astype(BF16)
    out[16:32, :] = got[...]


def joint_kernel(share, other, sent, got, after, out):
    out[0:16, :] = share[128:144, :]
    out[16:32, :] = other[128:144, :]
    out[32:48, :] = got[0:16, :]
    mine, peer = sent[16:32, :].astype(F32)[:8], got[16:32, :].astype(F32)[:8]
    out[48:64, :] = jnp.concatenate([mine, peer], axis=0).astype(BF16)


def far_join_kernel(sent, got, out):
    out[0:32, :] = got[0:32, :]
    for level in (1, 2):
        to, at = level * 32, 16 + level * 16
        out[to : to + 16, :] = sent[at : at + 16, :]
        out[to + 16 : to + 32, :] = got[at : at + 16, :]


def near_join_kernel(sent, got, out):
    out[0:32, :] = sent[64:96, :]
    out[32:64, :] = got[64:96, :]


def plane_join_kernel(first, second, out):
    out[0:64, :] = first[0:64, :]
    out[64:128, :] = second[...]


def row_join_kernel(a, b, c, d, *refs):
    out = refs[-1]
    for level in range(3):
        for step, piece in enumerate((a, b, c, d)):
            to = level * 128 + step * 32
            out[to : to + 32, :] = piece[level * 32 : (level + 1) * 32, :]


def columns(chunk):
    return pl.ds(pl.multiple_of(chunk * WIDTH, WIDTH), WIDTH)


def next_head(head):
    return head + 1 - 2 * (head % 2)


def stack_heads(query_t):
    head = lax.broadcasted_iota(jnp.int32, (WIDTH, BLOCK), 0) // 64
    zero = jnp.zeros_like(query_t)
    return jnp.concatenate([jnp.where(head == h, query_t, zero) for h in range(HEADS)], axis=1)


def turn(array):
    return array.astype(F32).T.astype(BF16)


def bias_kernel(gate, out):
    seq = lax.axis_index("seq")
    for b in range(4):
        for level in range(8):
            used = gate[b : b + 1, level : level + 1] == 1
            bias = jnp.where(used, jnp.float32(level * LOG_TWO), jnp.float32(NEG))
            if level >= 2:
                bit = lax.shift_right_logical(seq, level - 2) % 2
                bias = jnp.where(bit == 1, bias, jnp.float32(NEG))
            out[b * 8 + level : b * 8 + level + 1, :] = jnp.broadcast_to(bias, (1, BLOCK))


def gate_bias(bias, block, level):
    return bias[block * 8 + level : block * 8 + level + 1, :]


def attend(query_t, keys, values_t, biases, mask, old, old_top, old_total):
    scores = dot(keys, stack_heads(query_t))
    outs, tops, totals = [], [], []
    for h in range(HEADS):
        lanes = slice(h * BLOCK, (h + 1) * BLOCK)
        pieces = [scores[i * BLOCK : (i + 1) * BLOCK, lanes] for i in range(len(biases))]
        if mask is not None:
            pieces[0] = pieces[0] + mask
        top = None if old_top is None else old_top[:, lanes]
        for piece, bias in zip(pieces, biases):
            high = jnp.max(piece, axis=0, keepdims=True) + bias
            top = high if top is None else jnp.maximum(top, high)
        expo = [jnp.exp(piece - (top - bias)) for piece, bias in zip(pieces, biases)]
        total = sum(jnp.sum(piece, axis=0, keepdims=True) for piece in expo)
        weights = jnp.concatenate([piece.astype(BF16) for piece in expo], axis=0)
        rows = slice(h * 64, (h + 1) * 64)
        out = dot(values_t[rows, :], weights)
        if old is not None:
            scale = jnp.exp(old_top[:, lanes] - top)
            out = out + old[rows, :] * scale
            total = total + old_total[:, lanes] * scale
        outs.append(out)
        tops.append(top)
        totals.append(total)
    return outs, tops, totals


def own_half(half, gate, qt, kv, vt, l1, acc, ml):
    key = lax.broadcasted_iota(jnp.int32, (BLOCK, BLOCK), 0)
    row = lax.broadcasted_iota(jnp.int32, (BLOCK, BLOCK), 1)
    causal = jnp.where(key <= row, 0.0, NEG).astype(F32)
    if half:
        l1_t = turn(l1[:, WIDTH:])
    for step in range(2):
        b = half * 2 + step
        rows = slice(b * BLOCK, (b + 1) * BLOCK)
        keys = [kv[rows, :WIDTH]]
        values = [vt[:, rows]]
        biases = [jnp.float32(0.0)]
        if b & 1:
            before = slice((b - 1) * BLOCK, b * BLOCK)
            keys.append(kv[before, :WIDTH])
            values.append(vt[:, before])
            biases.append(gate_bias(gate, b, 0))
        if b & 2:
            keys.append(l1[:, :WIDTH])
            values.append(l1_t)
            biases.append(gate_bias(gate, b, 1))
        keys, values = jnp.concatenate(keys, axis=0), jnp.concatenate(values, axis=1)
        outs, tops, totals = attend(qt[:, rows], keys, values, biases, causal, None, None, None)
        acc[:, step * BLOCK : (step + 1) * BLOCK] = jnp.concatenate(outs, axis=0)
        ml[step : step + 1, :] = jnp.concatenate(tops, axis=1)
        ml[4 + step : 5 + step, :] = jnp.concatenate(totals, axis=1)


def own_blocks(gate, tok, wq, kv, l1, qt, acc0, ml0, acc1, ml1):
    query = dot(tok[...], wq[...]).astype(BF16).astype(F32) * 0.125
    query_t = query.T.astype(BF16)
    qt[...] = query_t
    values_t = turn(kv[:, WIDTH:])
    own_half(0, gate, query_t, kv, values_t, l1, acc0, ml0)
    own_half(1, gate, query_t, kv, values_t, l1, acc1, ml1)


def high_plane():
    return lax.axis_index("seq") >= 32


def early_kernel(gate, tok, wq, kv, l1, *outs):
    @pl.when(jnp.logical_not(high_plane()))
    def _():
        own_blocks(gate, tok, wq, kv, l1, *outs)


def late_kernel(gate, tok, wq, kv, l1, *refs):
    early, outs = refs[:5], refs[-5:]

    @pl.when(high_plane())
    def _():
        own_blocks(gate, tok, wq, kv, l1, *outs)

    @pl.when(jnp.logical_not(high_plane()))
    def _():
        for source, out in zip(early, outs):
            out[...] = source[...]


def level_biases(bias, block, first):
    return [gate_bias(bias, block, level) for level in range(first, first + 3)]


def cross(b, first, gate, qt, acc, ml, keys, values_t):
    step = b % 2
    biases = level_biases(gate, b, first)
    old = (acc[:, step * BLOCK : (step + 1) * BLOCK], ml[step : step + 1, :], ml[4 + step : 5 + step, :])
    return attend(qt[:, b * BLOCK : (b + 1) * BLOCK], keys, values_t, biases, None, *old)


def plane_kernel(gate, qt, acc0, ml0, acc1, ml1, share, first, second, other, *refs):
    outs_refs = refs[-4:]
    pieces = [share[0:128, :], first[0:64, :], other[0:64, :], second[...], other[64:128, :]]
    keys = jnp.concatenate([piece[:, :WIDTH] for piece in pieces], axis=0)
    values_t = turn(jnp.concatenate([piece[:, WIDTH:] for piece in pieces], axis=0))
    for b in range(4):
        half, step = b // 2, b % 2
        acc, ml = ((acc0, ml0), (acc1, ml1))[half]
        acc_out, ml_out = outs_refs[2 * half : 2 * half + 2]
        outs, tops, totals = cross(b, 2, gate, qt, acc, ml, keys, values_t)
        acc_out[:, step * BLOCK : (step + 1) * BLOCK] = jnp.concatenate(outs, axis=0)
        ml_out[step : step + 1, :] = jnp.concatenate(tops, axis=1)
        ml_out[4 + step : 5 + step, :] = jnp.concatenate(totals, axis=1)


def far_kernel(half, gate, qt, acc, ml, mine, other, after, att):
    rows = jnp.where(my_core() == 1, mine[...], other[...])
    keys = rows[:, :WIDTH]
    values_t = turn(rows[:, WIDTH:])
    for step in range(2):
        outs, _, totals = cross(half * 2 + step, 5, gate, qt, acc, ml, keys, values_t)
        outs = [out / total for out, total in zip(outs, totals)]
        turned = jnp.concatenate(outs, axis=0).T.astype(BF16)
        att[step * BLOCK : (step + 1) * BLOCK, :] = turned


def project_kernel(half, mine_att, peer_att, mine_w, peer_w, keep, send):
    head = lax.axis_index("head")
    other = 3 - head if half == 0 else next_head(head)
    for chunk, part, ref in ((other, slice(WIDTH, 2 * WIDTH), send), (head, slice(0, WIDTH), keep)):
        total = dot(mine_att[...], mine_w[:, columns(chunk)]) + dot(peer_att[...], peer_w[:, part])
        ref[...] = total.astype(ref.dtype)


VMEM = pl.BlockSpec(memory_space=pltpu.VMEM)
ANY = pl.BlockSpec(memory_space=pl.ANY)
HBM = pl.BlockSpec(memory_space=pltpu.HBM)


def call(kernel, args, outs, flops, unread=0):
    return pl.pallas_call(
        kernel,
        name=getattr(kernel, "func", kernel).__name__,
        out_shape=[jax.ShapeDtypeStruct(shape, dtype) for shape, dtype in outs],
        in_specs=[VMEM] * (len(args) - unread) + [ANY] * unread,
        out_specs=[VMEM] * len(outs),
        compiler_params=pltpu.CompilerParams(vmem_limit_bytes=24 * 1024 * 1024),
        cost_estimate=pl.CostEstimate(flops=flops, bytes_accessed=1000, transcendentals=0),
    )(*args)


def move(array, pairs, name):
    with jax.named_scope(name):
        return lax.ppermute(array, "seq", pairs)


def hub(array, to, idle, name):
    far = [(index(z, x, 1), index(*to(z, x), 1)) for z, x, c in CHIPS if c]
    near = [(index(z, x, 0), index(*idle(z, x), 0)) for z, x, c in CHIPS if not c]
    return move(array, far + near, name)


def idle_x(z, x):
    return z, x ^ 1


def idle_z(z, x):
    return z ^ 1, x


def across(array, bit, name):
    return move(array, [(index(z, x, c), index(z, x ^ bit, c)) for z, x, c in CHIPS], name)


def swap(array, name):
    return move(array, [(index(z, x, c), index(z, x, 1 - c)) for z, x, c in CHIPS], name)


PAIR_NEXT = [(0, 1), (1, 0), (2, 3), (3, 2)]
PAIR_FAR = [(0, 3), (3, 0), (1, 2), (2, 1)]


COST = 10**6


def shards(tokens, wq, wk, wv, wo, gate):
    rows = lambda n: ((n, 2 * WIDTH), BF16)
    kv, l1, e1, share, to_next, to_far = pl.pallas_call(
        load_kernel,
        name="load_kernel",
        out_shape=[
            jax.ShapeDtypeStruct(shape, BF16)
            for shape in ((512, 512), (128, 512), (96, 512), (176, 512))
            + ((WIDTH, 512),) * 2
        ],
        in_specs=[HBM] * 4,
        out_specs=[VMEM] * 6,
        scratch_shapes=[
            pltpu.VMEM((512, 1024), BF16),
            pltpu.VMEM((1024, WIDTH), BF16),
            pltpu.VMEM((1024, WIDTH), BF16),
            pltpu.SemaphoreType.DMA((8,)),
        ],
        compiler_params=pltpu.CompilerParams(vmem_limit_bytes=52 * 1024 * 1024),
        cost_estimate=pl.CostEstimate(flops=COST, bytes_accessed=1000, transcendentals=0),
    )(tokens, wk, wv, wo)
    share_other = swap(share, "swap_share")
    first = across(e1, 1, "across_one")
    state = [((WIDTH, 256), F32), ((8, 512), F32)]
    held = [((WIDTH, 512), BF16)] + state * 2
    (gate,) = call(bias_kernel, (gate,), [((32, BLOCK), F32)], COST)
    early = call(early_kernel, (gate, tokens, wq, kv, l1), held, COST)
    (pay,) = call(mirror_kernel, (share, share_other, early[2]), [rows(16)], COST, unread=1)
    far5 = hub(pay, lambda z, x: (7 - z, x), idle_x, "planes_mirror")
    qt, acc0, ml0, acc1, ml1 = call(
        late_kernel, (gate, tokens, wq, kv, l1, *early, pay), held, COST, unread=1
    )
    own = [(acc0, ml0), (acc1, ml1)]
    first, ml = lax.optimization_barrier((first, own[1][1]))
    own[1] = (own[1][0], ml)
    (near,) = call(near_join_kernel, (e1, first), [rows(64)], COST)
    second = across(near, 2, "across_two")
    (pay,) = call(
        two_kernel, (share, share_other, far5, own[0][1], own[1][1]), [rows(32)], COST, unread=2
    )
    got = hub(pay, lambda z, x: (z ^ 2, x), idle_x, "planes_two")
    (pay,) = call(
        joint_kernel, (share, share_other, pay, got, own[0][1]), [rows(64)], COST, unread=1
    )
    got = hub(pay, lambda z, x: (z ^ 1, x), idle_x, "planes_one")
    (far,) = call(far_join_kernel, (pay, got), [rows(96)], COST)
    (near,) = call(plane_join_kernel, (first, second), [rows(128)], COST)
    other = swap(near, "swap_near")
    far, to_far, to_next = lax.optimization_barrier((far, to_far, to_next))
    w_next = lax.ppermute(to_next, "head", PAIR_NEXT)
    w_far = lax.ppermute(to_far, "head", PAIR_FAR)
    acc0, ml0, acc1, ml1 = call(
        plane_kernel,
        (gate, qt, *own[0], *own[1], share_other, first, second, other),
        state * 2,
        COST,
    )
    others = [hub(far, lambda z, x, shift=shift: (z, x + shift), idle_z, "along") for shift in (1, -1, 2)]
    (far,) = call(row_join_kernel, (far, *others, ml0, w_next, w_far), [rows(384)], COST, unread=3)
    far_other = swap(far, "swap_far")
    held = ((acc0, ml0), (acc1, ml1))
    halves = []
    for half in range(2):
        after = far_other if half == 0 else halves[0]
        (att,) = call(
            functools.partial(far_kernel, half),
            (gate, qt, *held[half], far, far_other, after),
            [((256, WIDTH), BF16)],
            COST,
            unread=1,
        )
        halves.append(att)
    out = []
    pairs = (PAIR_NEXT, PAIR_FAR)
    for half in range(2):
        peer = lax.ppermute(halves[half], "head", pairs[half])
        keep, send = call(
            functools.partial(project_kernel, half),
            (halves[half], peer, wo, (w_next, w_far)[half]),
            [((256, WIDTH), F32), ((256, WIDTH), BF16)],
            COST,
        )
        out.append(keep + lax.ppermute(send, "head", pairs[1 - half]).astype(F32))
    return jnp.concatenate(out, axis=0).astype(BF16)


def solution(mesh):
    placed = (
        P("seq", None),
        P(None, "head"),
        P(None, "head"),
        P(None, "head"),
        P("head", None),
        P("seq", None),
    )
    return jax.shard_map(
        shards, mesh=mesh, in_specs=placed, out_specs=P("seq", "head"), check_vma=False
    )
```

```python
import functools
import math

import jax
import jax.numpy as jnp
from jax import lax
from jax.experimental import pallas as pl
from jax.experimental.pallas import tpu as pltpu
from jax.sharding import PartitionSpec as P

LOG_TWO = math.log(2.0)
NEG = -1e30
BLOCK = 128
WIDTH = 256
HEADS = 4
F32 = jnp.float32
BF16 = jnp.bfloat16

Z, X, C = 8, 4, 2


def index(z, x, c):
    return (z % Z) * 8 + (x % X) * 2 + c


CHIPS = [(z, x, c) for z in range(Z) for x in range(X) for c in range(C)]


def dot(a, b):
    return lax.dot_general(a, b, (((1,), (0,)), ((), ())), preferred_element_type=F32)


def pool_rows(rows, level):
    token = lax.broadcasted_iota(jnp.int32, (rows, 512), 1)
    row = lax.broadcasted_iota(jnp.int32, (rows, 512), 0)
    inverse = jnp.float32(0.0)
    for each in range(1, 8):
        inverse = jnp.where(level == each, jnp.float32(2.0**-each), inverse)
    hit = lax.shift_right_logical(token, jnp.full((rows, 512), level, jnp.int32)) == row
    return jnp.where(hit, inverse, 0.0).astype(BF16)


def my_core():
    return lax.axis_index("seq") % 2


def load_kernel(
    tok_hbm, wk_hbm, wv_hbm, wo_hbm,
    kv, l1, e1, share, to_next, to_far,
    tok, wk, wv, sems,
):
    head = lax.axis_index("head")
    near, far = next_head(head), 3 - head
    pairs = [(wk_hbm, wk)]
    pairs += [(tok_hbm.at[pl.ds(i * 256, 256)], tok.at[pl.ds(i * 256, 256)]) for i in range(2)]
    pairs.append((wv_hbm, wv))
    for out, first, second in ((to_next, near, 3 - near), (to_far, far, next_head(far))):
        pairs.append((wo_hbm.at[:, columns(first)], out.at[:, pl.ds(0, WIDTH)]))
        pairs.append((wo_hbm.at[:, columns(second)], out.at[:, pl.ds(WIDTH, WIDTH)]))
    copies = [pltpu.make_async_copy(*pair, sems.at[i]) for i, pair in enumerate(pairs)]
    for copy in copies:
        copy.start()
    parts = [
        pool_rows(n, level)
        for n, level in ((128, 1), (64, 3), (32, 4), (128, 2), (16, 5), (16, 6), (16, 7))
    ]
    for copy in copies[:3]:
        copy.wait()
    keys = dot(tok[...], wk[...]).astype(BF16)
    copies[3].wait()
    values = dot(tok[...], wv[...]).astype(BF16)
    both = jnp.concatenate([keys, values], axis=1)
    kv[...] = both
    pooled = dot(jnp.concatenate(parts, axis=0), both)
    l1[...] = pooled[0:128].astype(BF16)
    e1[...] = pooled[128:224].astype(BF16)
    share[...] = pooled[224:400].astype(BF16)
    for copy in copies[4:]:
        copy.wait()


def mirror_kernel(share, other, after, out):
    own, far = share[160:176, :].astype(F32)[:4], other[160:176, :].astype(F32)[:4]
    out[...] = jnp.concatenate([own, far, own, far], axis=0).astype(BF16)


def two_kernel(share, other, got, after0, after1, out):
    own, far = share[144:160, :].astype(F32)[:8], other[144:160, :].astype(F32)[:8]
    out[0:16, :] = jnp.concatenate([own, far], axis=0).astype(BF16)
    out[16:32, :] = got[...]


def joint_kernel(share, other, sent, got, after, out):
    out[0:16, :] = share[128:144, :]
    out[16:32, :] = other[128:144, :]
    out[32:48, :] = got[0:16, :]
    mine, peer = sent[16:32, :].astype(F32)[:8], got[16:32, :].astype(F32)[:8]
    out[48:64, :] = jnp.concatenate([mine, peer], axis=0).astype(BF16)


def far_join_kernel(sent, got, w_next, w_far, out):
    out[0:32, :] = got[0:32, :]
    for level in (1, 2):
        to, at = level * 32, 16 + level * 16
        out[to : to + 16, :] = sent[at : at + 16, :]
        out[to + 16 : to + 32, :] = got[at : at + 16, :]


def near_join_kernel(sent, got, out):
    out[0:32, :] = sent[64:96, :]
    out[32:64, :] = got[64:96, :]


def plane_join_kernel(first, second, out):
    out[0:64, :] = first[0:64, :]
    out[64:128, :] = second[...]


def row_join_kernel(a, b, c, d, after, out):
    for level in range(3):
        for step, piece in enumerate((a, b, c, d)):
            to = level * 128 + step * 32
            out[to : to + 32, :] = piece[level * 32 : (level + 1) * 32, :]


def columns(chunk):
    return pl.ds(pl.multiple_of(chunk * WIDTH, WIDTH), WIDTH)


def next_head(head):
    return head + 1 - 2 * (head % 2)


def stack_heads(query_t):
    head = lax.broadcasted_iota(jnp.int32, (WIDTH, BLOCK), 0) // 64
    zero = jnp.zeros_like(query_t)
    return jnp.concatenate([jnp.where(head == h, query_t, zero) for h in range(HEADS)], axis=1)


def turn(array):
    return array.astype(F32).T.astype(BF16)


def bias_kernel(gate, out):
    seq = lax.axis_index("seq")
    for b in range(4):
        for level in range(8):
            used = gate[b : b + 1, level : level + 1] == 1
            bias = jnp.where(used, jnp.float32(level * LOG_TWO), jnp.float32(NEG))
            if level >= 2:
                bit = lax.shift_right_logical(seq, level - 2) % 2
                bias = jnp.where(bit == 1, bias, jnp.float32(NEG))
            out[b * 8 + level : b * 8 + level + 1, :] = jnp.broadcast_to(bias, (1, BLOCK))


def gate_bias(bias, block, level):
    return bias[block * 8 + level : block * 8 + level + 1, :]


def attend(query_t, keys, values_t, biases, mask, old, old_top, old_total):
    scores = dot(keys, stack_heads(query_t))
    outs, tops, totals = [], [], []
    for h in range(HEADS):
        lanes = slice(h * BLOCK, (h + 1) * BLOCK)
        pieces = [scores[i * BLOCK : (i + 1) * BLOCK, lanes] for i in range(len(biases))]
        if mask is not None:
            pieces[0] = pieces[0] + mask
        top = None if old_top is None else old_top[:, lanes]
        for piece, bias in zip(pieces, biases):
            high = jnp.max(piece, axis=0, keepdims=True) + bias
            top = high if top is None else jnp.maximum(top, high)
        expo = [jnp.exp(piece - (top - bias)) for piece, bias in zip(pieces, biases)]
        total = sum(jnp.sum(piece, axis=0, keepdims=True) for piece in expo)
        weights = jnp.concatenate([piece.astype(BF16) for piece in expo], axis=0)
        rows = slice(h * 64, (h + 1) * 64)
        out = dot(values_t[rows, :], weights)
        if old is not None:
            scale = jnp.exp(old_top[:, lanes] - top)
            out = out + old[rows, :] * scale
            total = total + old_total[:, lanes] * scale
        outs.append(out)
        tops.append(top)
        totals.append(total)
    return outs, tops, totals


def own_half(half, gate, qt, kv, vt, l1, acc, ml):
    key = lax.broadcasted_iota(jnp.int32, (BLOCK, BLOCK), 0)
    row = lax.broadcasted_iota(jnp.int32, (BLOCK, BLOCK), 1)
    causal = jnp.where(key <= row, 0.0, NEG).astype(F32)
    if half:
        l1_t = turn(l1[:, WIDTH:])
    for step in range(2):
        b = half * 2 + step
        rows = slice(b * BLOCK, (b + 1) * BLOCK)
        keys = [kv[rows, :WIDTH]]
        values = [vt[:, rows]]
        biases = [jnp.float32(0.0)]
        if b & 1:
            before = slice((b - 1) * BLOCK, b * BLOCK)
            keys.append(kv[before, :WIDTH])
            values.append(vt[:, before])
            biases.append(gate_bias(gate, b, 0))
        if b & 2:
            keys.append(l1[:, :WIDTH])
            values.append(l1_t)
            biases.append(gate_bias(gate, b, 1))
        keys, values = jnp.concatenate(keys, axis=0), jnp.concatenate(values, axis=1)
        outs, tops, totals = attend(qt[:, rows], keys, values, biases, causal, None, None, None)
        acc[:, step * BLOCK : (step + 1) * BLOCK] = jnp.concatenate(outs, axis=0)
        ml[step : step + 1, :] = jnp.concatenate(tops, axis=1)
        ml[4 + step : 5 + step, :] = jnp.concatenate(totals, axis=1)


def own_blocks(gate, tok, wq, kv, l1, qt, acc0, ml0, acc1, ml1):
    query = dot(tok[...], wq[...]).astype(BF16).astype(F32) * 0.125
    query_t = query.T.astype(BF16)
    qt[...] = query_t
    values_t = turn(kv[:, WIDTH:])
    own_half(0, gate, query_t, kv, values_t, l1, acc0, ml0)
    own_half(1, gate, query_t, kv, values_t, l1, acc1, ml1)


def high_plane():
    return lax.axis_index("seq") >= 32


def early_kernel(gate, tok, wq, kv, l1, *outs):
    @pl.when(jnp.logical_not(high_plane()))
    def _():
        own_blocks(gate, tok, wq, kv, l1, *outs)


def late_kernel(gate, tok, wq, kv, l1, *refs):
    early, outs = refs[:5], refs[-5:]

    @pl.when(high_plane())
    def _():
        own_blocks(gate, tok, wq, kv, l1, *outs)

    @pl.when(jnp.logical_not(high_plane()))
    def _():
        for source, out in zip(early, outs):
            out[...] = source[...]


def level_biases(bias, block, first):
    return [gate_bias(bias, block, level) for level in range(first, first + 3)]


def cross(b, first, gate, qt, acc, ml, keys, values_t):
    step = b % 2
    biases = level_biases(gate, b, first)
    old = (acc[:, step * BLOCK : (step + 1) * BLOCK], ml[step : step + 1, :], ml[4 + step : 5 + step, :])
    return attend(qt[:, b * BLOCK : (b + 1) * BLOCK], keys, values_t, biases, None, *old)


def plane_kernel(gate, qt, acc0, ml0, acc1, ml1, share, first, second, other, *refs):
    outs_refs = refs[-4:]
    pieces = [share[0:128, :], first[0:64, :], other[0:64, :], second[...], other[64:128, :]]
    keys = jnp.concatenate([piece[:, :WIDTH] for piece in pieces], axis=0)
    values_t = turn(jnp.concatenate([piece[:, WIDTH:] for piece in pieces], axis=0))
    for b in range(4):
        half, step = b // 2, b % 2
        acc, ml = ((acc0, ml0), (acc1, ml1))[half]
        acc_out, ml_out = outs_refs[2 * half : 2 * half + 2]
        outs, tops, totals = cross(b, 2, gate, qt, acc, ml, keys, values_t)
        acc_out[:, step * BLOCK : (step + 1) * BLOCK] = jnp.concatenate(outs, axis=0)
        ml_out[step : step + 1, :] = jnp.concatenate(tops, axis=1)
        ml_out[4 + step : 5 + step, :] = jnp.concatenate(totals, axis=1)


def far_kernel(half, gate, qt, acc, ml, mine, other, after, att):
    rows = jnp.where(my_core() == 1, mine[...], other[...])
    keys = rows[:, :WIDTH]
    values_t = turn(rows[:, WIDTH:])
    for step in range(2):
        outs, _, totals = cross(half * 2 + step, 5, gate, qt, acc, ml, keys, values_t)
        outs = [out / total for out, total in zip(outs, totals)]
        turned = jnp.concatenate(outs, axis=0).T.astype(BF16)
        att[step * BLOCK : (step + 1) * BLOCK, :] = turned


def project_kernel(half, mine_att, peer_att, mine_w, peer_w, keep, send):
    head = lax.axis_index("head")
    other = 3 - head if half == 0 else next_head(head)
    for chunk, part, ref in ((other, slice(WIDTH, 2 * WIDTH), send), (head, slice(0, WIDTH), keep)):
        total = dot(mine_att[...], mine_w[:, columns(chunk)]) + dot(peer_att[...], peer_w[:, part])
        ref[...] = total.astype(ref.dtype)


VMEM = pl.BlockSpec(memory_space=pltpu.VMEM)
ANY = pl.BlockSpec(memory_space=pl.ANY)
HBM = pl.BlockSpec(memory_space=pltpu.HBM)


def call(kernel, args, outs, flops, unread=0):
    return pl.pallas_call(
        kernel,
        name=getattr(kernel, "func", kernel).__name__,
        out_shape=[jax.ShapeDtypeStruct(shape, dtype) for shape, dtype in outs],
        in_specs=[VMEM] * (len(args) - unread) + [ANY] * unread,
        out_specs=[VMEM] * len(outs),
        compiler_params=pltpu.CompilerParams(vmem_limit_bytes=24 * 1024 * 1024),
        cost_estimate=pl.CostEstimate(flops=flops, bytes_accessed=1000, transcendentals=0),
    )(*args)


def move(array, pairs, name):
    with jax.named_scope(name):
        return lax.ppermute(array, "seq", pairs)


def hub(array, to, idle, name):
    far = [(index(z, x, 1), index(*to(z, x), 1)) for z, x, c in CHIPS if c]
    near = [(index(z, x, 0), index(*idle(z, x), 0)) for z, x, c in CHIPS if not c]
    return move(array, far + near, name)


def idle_x(z, x):
    return z, x ^ 1


def idle_z(z, x):
    return z ^ 1, x


def across(array, bit, name):
    return move(array, [(index(z, x, c), index(z, x ^ bit, c)) for z, x, c in CHIPS], name)


def swap(array, name):
    return move(array, [(index(z, x, c), index(z, x, 1 - c)) for z, x, c in CHIPS], name)


PAIR_NEXT = [(0, 1), (1, 0), (2, 3), (3, 2)]
PAIR_FAR = [(0, 3), (3, 0), (1, 2), (2, 1)]


COST = 10**6


def shards(tokens, wq, wk, wv, wo, gate):
    rows = lambda n: ((n, 2 * WIDTH), BF16)
    kv, l1, e1, share, to_next, to_far = pl.pallas_call(
        load_kernel,
        name="load_kernel",
        out_shape=[
            jax.ShapeDtypeStruct(shape, BF16)
            for shape in ((512, 512), (128, 512), (96, 512), (176, 512))
            + ((WIDTH, 512),) * 2
        ],
        in_specs=[HBM] * 4,
        out_specs=[VMEM] * 6,
        scratch_shapes=[
            pltpu.VMEM((512, 1024), BF16),
            pltpu.VMEM((1024, WIDTH), BF16),
            pltpu.VMEM((1024, WIDTH), BF16),
            pltpu.SemaphoreType.DMA((8,)),
        ],
        compiler_params=pltpu.CompilerParams(vmem_limit_bytes=105 * 512 * 1024),
        cost_estimate=pl.CostEstimate(flops=COST, bytes_accessed=1000, transcendentals=0),
    )(tokens, wk, wv, wo)
    w_next = lax.ppermute(to_next, "head", PAIR_NEXT)
    w_far = lax.ppermute(to_far, "head", PAIR_FAR)
    share_other = swap(share, "swap_share")
    first = across(e1, 1, "across_one")
    state = [((WIDTH, 256), F32), ((8, 512), F32)]
    held = [((WIDTH, 512), BF16)] + state * 2
    (gate,) = call(bias_kernel, (gate,), [((32, BLOCK), F32)], COST)
    early = call(early_kernel, (gate, tokens, wq, kv, l1), held, COST)
    (pay,) = call(mirror_kernel, (share, share_other, early[2]), [rows(16)], COST, unread=1)
    far5 = hub(pay, lambda z, x: (7 - z, x), idle_x, "planes_mirror")
    qt, acc0, ml0, acc1, ml1 = call(
        late_kernel, (gate, tokens, wq, kv, l1, *early, pay), held, COST, unread=1
    )
    own = [(acc0, ml0), (acc1, ml1)]
    first, ml = lax.optimization_barrier((first, own[1][1]))
    own[1] = (own[1][0], ml)
    (near,) = call(near_join_kernel, (e1, first), [rows(64)], COST)
    second = across(near, 2, "across_two")
    (pay,) = call(
        two_kernel, (share, share_other, far5, own[0][1], own[1][1]), [rows(32)], COST, unread=2
    )
    got = hub(pay, lambda z, x: (z ^ 2, x), idle_x, "planes_two")
    (pay,) = call(
        joint_kernel, (share, share_other, pay, got, own[0][1]), [rows(64)], COST, unread=1
    )
    got = hub(pay, lambda z, x: (z ^ 1, x), idle_x, "planes_one")
    (far,) = call(far_join_kernel, (pay, got, w_next, w_far), [rows(96)], COST, unread=2)
    (near,) = call(plane_join_kernel, (first, second), [rows(128)], COST)
    other = swap(near, "swap_near")
    acc0, ml0, acc1, ml1 = call(
        plane_kernel,
        (gate, qt, *own[0], *own[1], share_other, first, second, other),
        state * 2,
        COST,
    )
    others = [hub(far, lambda z, x, shift=shift: (z, x + shift), idle_z, "along") for shift in (1, -1, 2)]
    (far,) = call(row_join_kernel, (far, *others, ml0), [rows(384)], COST, unread=1)
    far_other = swap(far, "swap_far")
    held = ((acc0, ml0), (acc1, ml1))
    halves = []
    for half in range(2):
        after = far_other if half == 0 else halves[0]
        (att,) = call(
            functools.partial(far_kernel, half),
            (gate, qt, *held[half], far, far_other, after),
            [((256, WIDTH), BF16)],
            COST,
            unread=1,
        )
        halves.append(att)
    out = []
    pairs = (PAIR_NEXT, PAIR_FAR)
    for half in range(2):
        peer = lax.ppermute(halves[half], "head", pairs[half])
        keep, send = call(
            functools.partial(project_kernel, half),
            (halves[half], peer, wo, (w_next, w_far)[half]),
            [((256, WIDTH), F32), ((256, WIDTH), BF16)],
            COST,
        )
        out.append(keep + lax.ppermute(send, "head", pairs[1 - half]).astype(F32))
    return jnp.concatenate(out, axis=0).astype(BF16)


def solution(mesh):
    placed = (
        P("seq", None),
        P(None, "head"),
        P(None, "head"),
        P(None, "head"),
        P("head", None),
        P("seq", None),
    )
    return jax.shard_map(
        shards, mesh=mesh, in_specs=placed, out_specs=P("seq", "head"), check_vma=False
    )
```

```python
import functools
import math

import jax
import jax.numpy as jnp
from jax import lax
from jax.experimental import pallas as pl
from jax.experimental.pallas import tpu as pltpu
from jax.sharding import PartitionSpec as P

LOG_TWO = math.log(2.0)
NEG = -1e30
BLOCK = 128
WIDTH = 256
HEADS = 4
F32 = jnp.float32
BF16 = jnp.bfloat16

Z, X, C = 8, 4, 2


def index(z, x, c):
    return (z % Z) * 8 + (x % X) * 2 + c


CHIPS = [(z, x, c) for z in range(Z) for x in range(X) for c in range(C)]


def dot(a, b):
    return lax.dot_general(a, b, (((1,), (0,)), ((), ())), preferred_element_type=F32)


def pool_rows(rows, level):
    token = lax.broadcasted_iota(jnp.int32, (rows, 512), 1)
    row = lax.broadcasted_iota(jnp.int32, (rows, 512), 0)
    inverse = jnp.float32(0.0)
    for each in range(1, 8):
        inverse = jnp.where(level == each, jnp.float32(2.0**-each), inverse)
    hit = lax.shift_right_logical(token, jnp.full((rows, 512), level, jnp.int32)) == row
    return jnp.where(hit, inverse, 0.0).astype(BF16)


def my_core():
    return lax.axis_index("seq") % 2


def load_kernel(
    tok_hbm, wk_hbm, wv_hbm, wo_hbm,
    kv, l1, e1, share, to_next, to_far,
    tok, wk, wv, sems,
):
    head = lax.axis_index("head")
    near, far = next_head(head), 3 - head
    pairs = [(wk_hbm, wk)]
    pairs += [(tok_hbm.at[pl.ds(i * 256, 256)], tok.at[pl.ds(i * 256, 256)]) for i in range(2)]
    pairs.append((wv_hbm, wv))
    for out, first, second in ((to_next, near, 3 - near), (to_far, far, next_head(far))):
        pairs.append((wo_hbm.at[:, columns(first)], out.at[:, pl.ds(0, WIDTH)]))
        pairs.append((wo_hbm.at[:, columns(second)], out.at[:, pl.ds(WIDTH, WIDTH)]))
    copies = [pltpu.make_async_copy(*pair, sems.at[i]) for i, pair in enumerate(pairs)]
    for copy in copies:
        copy.start()
    parts = [
        pool_rows(n, level)
        for n, level in ((128, 1), (64, 3), (32, 4), (128, 2), (16, 5), (16, 6), (16, 7))
    ]
    for copy in copies[:3]:
        copy.wait()
    keys = dot(tok[...], wk[...]).astype(BF16)
    copies[3].wait()
    values = dot(tok[...], wv[...]).astype(BF16)
    both = jnp.concatenate([keys, values], axis=1)
    kv[...] = both
    pooled = dot(jnp.concatenate(parts, axis=0), both)
    l1[...] = pooled[0:128].astype(BF16)
    e1[...] = pooled[128:224].astype(BF16)
    share[...] = pooled[224:400].astype(BF16)
    for copy in copies[4:]:
        copy.wait()


def mirror_kernel(share, other, after, out):
    own, far = share[160:176, :].astype(F32)[:4], other[160:176, :].astype(F32)[:4]
    out[...] = jnp.concatenate([own, far, own, far], axis=0).astype(BF16)


def two_kernel(share, other, got, after0, after1, out):
    own, far = share[144:160, :].astype(F32)[:8], other[144:160, :].astype(F32)[:8]
    out[0:16, :] = jnp.concatenate([own, far], axis=0).astype(BF16)
    out[16:32, :] = got[...]


def joint_kernel(share, other, sent, got, after, out):
    out[0:16, :] = share[128:144, :]
    out[16:32, :] = other[128:144, :]
    out[32:48, :] = got[0:16, :]
    mine, peer = sent[16:32, :].astype(F32)[:8], got[16:32, :].astype(F32)[:8]
    out[48:64, :] = jnp.concatenate([mine, peer], axis=0).astype(BF16)


def far_join_kernel(sent, got, w_next, w_far, out):
    out[0:32, :] = got[0:32, :]
    for level in (1, 2):
        to, at = level * 32, 16 + level * 16
        out[to : to + 16, :] = sent[at : at + 16, :]
        out[to + 16 : to + 32, :] = got[at : at + 16, :]


def near_join_kernel(sent, got, out):
    out[0:32, :] = sent[64:96, :]
    out[32:64, :] = got[64:96, :]


def plane_join_kernel(first, second, out):
    out[0:64, :] = first[0:64, :]
    out[64:128, :] = second[...]


def row_join_kernel(a, b, c, d, after, out):
    for level in range(3):
        for step, piece in enumerate((a, b, c, d)):
            to = level * 128 + step * 32
            out[to : to + 32, :] = piece[level * 32 : (level + 1) * 32, :]


def columns(chunk):
    return pl.ds(pl.multiple_of(chunk * WIDTH, WIDTH), WIDTH)


def next_head(head):
    return head + 1 - 2 * (head % 2)


def stack_heads(query_t):
    head = lax.broadcasted_iota(jnp.int32, (WIDTH, BLOCK), 0) // 64
    zero = jnp.zeros_like(query_t)
    return jnp.concatenate([jnp.where(head == h, query_t, zero) for h in range(HEADS)], axis=1)


def turn(array):
    return array.astype(F32).T.astype(BF16)


def bias_kernel(gate, out):
    seq = lax.axis_index("seq")
    for b in range(4):
        for level in range(8):
            used = gate[b : b + 1, level : level + 1] == 1
            bias = jnp.where(used, jnp.float32(level * LOG_TWO), jnp.float32(NEG))
            if level >= 2:
                bit = lax.shift_right_logical(seq, level - 2) % 2
                bias = jnp.where(bit == 1, bias, jnp.float32(NEG))
            out[b * 8 + level : b * 8 + level + 1, :] = jnp.broadcast_to(bias, (1, BLOCK))


def gate_bias(bias, block, level):
    return bias[block * 8 + level : block * 8 + level + 1, :]


def attend(query_t, keys, values_t, biases, mask, old, old_top, old_total):
    scores = dot(keys, stack_heads(query_t))
    outs, tops, totals = [], [], []
    for h in range(HEADS):
        lanes = slice(h * BLOCK, (h + 1) * BLOCK)
        pieces = [scores[i * BLOCK : (i + 1) * BLOCK, lanes] for i in range(len(biases))]
        if mask is not None:
            pieces[0] = pieces[0] + mask
        top = None if old_top is None else old_top[:, lanes]
        for piece, bias in zip(pieces, biases):
            high = jnp.max(piece, axis=0, keepdims=True) + bias
            top = high if top is None else jnp.maximum(top, high)
        expo = [jnp.exp(piece - (top - bias)) for piece, bias in zip(pieces, biases)]
        total = sum(jnp.sum(piece, axis=0, keepdims=True) for piece in expo)
        weights = jnp.concatenate([piece.astype(BF16) for piece in expo], axis=0)
        rows = slice(h * 64, (h + 1) * 64)
        out = dot(values_t[rows, :], weights)
        if old is not None:
            scale = jnp.exp(old_top[:, lanes] - top)
            out = out + old[rows, :] * scale
            total = total + old_total[:, lanes] * scale
        outs.append(out)
        tops.append(top)
        totals.append(total)
    return outs, tops, totals


def own_half(half, gate, qt, kv, vt, l1, acc, ml):
    key = lax.broadcasted_iota(jnp.int32, (BLOCK, BLOCK), 0)
    row = lax.broadcasted_iota(jnp.int32, (BLOCK, BLOCK), 1)
    causal = jnp.where(key <= row, 0.0, NEG).astype(F32)
    if half:
        l1_t = turn(l1[:, WIDTH:])
    for step in range(2):
        b = half * 2 + step
        rows = slice(b * BLOCK, (b + 1) * BLOCK)
        keys = [kv[rows, :WIDTH]]
        values = [vt[:, rows]]
        biases = [jnp.float32(0.0)]
        if b & 1:
            before = slice((b - 1) * BLOCK, b * BLOCK)
            keys.append(kv[before, :WIDTH])
            values.append(vt[:, before])
            biases.append(gate_bias(gate, b, 0))
        if b & 2:
            keys.append(l1[:, :WIDTH])
            values.append(l1_t)
            biases.append(gate_bias(gate, b, 1))
        keys, values = jnp.concatenate(keys, axis=0), jnp.concatenate(values, axis=1)
        outs, tops, totals = attend(qt[:, rows], keys, values, biases, causal, None, None, None)
        acc[:, step * BLOCK : (step + 1) * BLOCK] = jnp.concatenate(outs, axis=0)
        ml[step : step + 1, :] = jnp.concatenate(tops, axis=1)
        ml[4 + step : 5 + step, :] = jnp.concatenate(totals, axis=1)


def own_blocks(gate, tok, wq, kv, l1, qt, acc0, ml0, acc1, ml1):
    query = dot(tok[...], wq[...]).astype(BF16).astype(F32) * 0.125
    query_t = query.T.astype(BF16)
    qt[...] = query_t
    values_t = turn(kv[:, WIDTH:])
    own_half(0, gate, query_t, kv, values_t, l1, acc0, ml0)
    own_half(1, gate, query_t, kv, values_t, l1, acc1, ml1)


def high_plane():
    return lax.axis_index("seq") >= 32


def early_kernel(gate, tok, wq, kv, l1, *outs):
    @pl.when(jnp.logical_not(high_plane()))
    def _():
        own_blocks(gate, tok, wq, kv, l1, *outs)


def late_kernel(gate, tok, wq, kv, l1, *refs):
    early, outs = refs[:5], refs[-5:]

    @pl.when(high_plane())
    def _():
        own_blocks(gate, tok, wq, kv, l1, *outs)

    @pl.when(jnp.logical_not(high_plane()))
    def _():
        for source, out in zip(early, outs):
            out[...] = source[...]


def level_biases(bias, block, first):
    return [gate_bias(bias, block, level) for level in range(first, first + 3)]


def cross(b, first, gate, qt, acc, ml, keys, values_t):
    step = b % 2
    biases = level_biases(gate, b, first)
    old = (acc[:, step * BLOCK : (step + 1) * BLOCK], ml[step : step + 1, :], ml[4 + step : 5 + step, :])
    return attend(qt[:, b * BLOCK : (b + 1) * BLOCK], keys, values_t, biases, None, *old)


def plane_kernel(gate, qt, acc0, ml0, acc1, ml1, share, first, second, other, *refs):
    outs_refs = refs[-4:]
    pieces = [share[0:128, :], first[0:64, :], other[0:64, :], second[...], other[64:128, :]]
    keys = jnp.concatenate([piece[:, :WIDTH] for piece in pieces], axis=0)
    values_t = turn(jnp.concatenate([piece[:, WIDTH:] for piece in pieces], axis=0))
    for b in range(4):
        half, step = b // 2, b % 2
        acc, ml = ((acc0, ml0), (acc1, ml1))[half]
        acc_out, ml_out = outs_refs[2 * half : 2 * half + 2]
        outs, tops, totals = cross(b, 2, gate, qt, acc, ml, keys, values_t)
        acc_out[:, step * BLOCK : (step + 1) * BLOCK] = jnp.concatenate(outs, axis=0)
        ml_out[step : step + 1, :] = jnp.concatenate(tops, axis=1)
        ml_out[4 + step : 5 + step, :] = jnp.concatenate(totals, axis=1)


def far_kernel(half, gate, qt, acc, ml, mine, other, after, att):
    rows = jnp.where(my_core() == 1, mine[...], other[...])
    keys = rows[:, :WIDTH]
    values_t = turn(rows[:, WIDTH:])
    for step in range(2):
        outs, _, totals = cross(half * 2 + step, 5, gate, qt, acc, ml, keys, values_t)
        outs = [out / total for out, total in zip(outs, totals)]
        turned = jnp.concatenate(outs, axis=0).T.astype(BF16)
        att[step * BLOCK : (step + 1) * BLOCK, :] = turned


def project_kernel(half, mine_att, peer_att, mine_w, peer_w, keep, send):
    head = lax.axis_index("head")
    other = 3 - head if half == 0 else next_head(head)
    for chunk, part, ref in ((other, slice(WIDTH, 2 * WIDTH), send), (head, slice(0, WIDTH), keep)):
        total = dot(mine_att[...], mine_w[:, columns(chunk)]) + dot(peer_att[...], peer_w[:, part])
        ref[...] = total.astype(ref.dtype)


VMEM = pl.BlockSpec(memory_space=pltpu.VMEM)
ANY = pl.BlockSpec(memory_space=pl.ANY)
HBM = pl.BlockSpec(memory_space=pltpu.HBM)


def call(kernel, args, outs, flops, unread=0):
    return pl.pallas_call(
        kernel,
        name=getattr(kernel, "func", kernel).__name__,
        out_shape=[jax.ShapeDtypeStruct(shape, dtype) for shape, dtype in outs],
        in_specs=[VMEM] * (len(args) - unread) + [ANY] * unread,
        out_specs=[VMEM] * len(outs),
        compiler_params=pltpu.CompilerParams(vmem_limit_bytes=24 * 1024 * 1024),
        cost_estimate=pl.CostEstimate(flops=flops, bytes_accessed=1000, transcendentals=0),
    )(*args)


def move(array, pairs, name):
    with jax.named_scope(name):
        return lax.ppermute(array, "seq", pairs)


def hub(array, to, idle, name):
    far = [(index(z, x, 1), index(*to(z, x), 1)) for z, x, c in CHIPS if c]
    near = [(index(z, x, 0), index(*idle(z, x), 0)) for z, x, c in CHIPS if not c]
    return move(array, far + near, name)


def idle_x(z, x):
    return z, x ^ 1


def idle_z(z, x):
    return z ^ 1, x


def idle_z_odd(z, x):
    return (z + 1 if z % 2 else z - 1) % Z, x


def across(array, bit, name):
    return move(array, [(index(z, x, c), index(z, x ^ bit, c)) for z, x, c in CHIPS], name)


def swap(array, name):
    return move(array, [(index(z, x, c), index(z, x, 1 - c)) for z, x, c in CHIPS], name)


PAIR_NEXT = [(0, 1), (1, 0), (2, 3), (3, 2)]
PAIR_FAR = [(0, 3), (3, 0), (1, 2), (2, 1)]


COST = 10**6


def shards(tokens, wq, wk, wv, wo, gate):
    rows = lambda n: ((n, 2 * WIDTH), BF16)
    kv, l1, e1, share, to_next, to_far = pl.pallas_call(
        load_kernel,
        name="load_kernel",
        out_shape=[
            jax.ShapeDtypeStruct(shape, BF16)
            for shape in ((512, 512), (128, 512), (96, 512), (176, 512))
            + ((WIDTH, 512),) * 2
        ],
        in_specs=[HBM] * 4,
        out_specs=[VMEM] * 6,
        scratch_shapes=[
            pltpu.VMEM((512, 1024), BF16),
            pltpu.VMEM((1024, WIDTH), BF16),
            pltpu.VMEM((1024, WIDTH), BF16),
            pltpu.SemaphoreType.DMA((8,)),
        ],
        compiler_params=pltpu.CompilerParams(vmem_limit_bytes=105 * 512 * 1024),
        cost_estimate=pl.CostEstimate(flops=COST, bytes_accessed=1000, transcendentals=0),
    )(tokens, wk, wv, wo)
    w_next = lax.ppermute(to_next, "head", PAIR_NEXT)
    w_far = lax.ppermute(to_far, "head", PAIR_FAR)
    share_other = swap(share, "swap_share")
    first = across(e1, 1, "across_one")
    state = [((WIDTH, 256), F32), ((8, 512), F32)]
    held = [((WIDTH, 512), BF16)] + state * 2
    (gate,) = call(bias_kernel, (gate,), [((32, BLOCK), F32)], COST)
    early = call(early_kernel, (gate, tokens, wq, kv, l1), held, COST)
    (pay,) = call(mirror_kernel, (share, share_other, early[2]), [rows(16)], COST, unread=1)
    far5 = hub(pay, lambda z, x: (z ^ 6, x), idle_x, "planes_mirror")
    qt, acc0, ml0, acc1, ml1 = call(
        late_kernel, (gate, tokens, wq, kv, l1, *early, pay), held, COST, unread=1
    )
    own = [(acc0, ml0), (acc1, ml1)]
    first, ml = lax.optimization_barrier((first, own[1][1]))
    own[1] = (own[1][0], ml)
    (near,) = call(near_join_kernel, (e1, first), [rows(64)], COST)
    second = across(near, 2, "across_two")
    (pay,) = call(
        two_kernel, (share, share_other, far5, own[0][1], own[1][1]), [rows(32)], COST, unread=2
    )
    got = hub(pay, lambda z, x: (z ^ 2, x), idle_x, "planes_two")
    (pay,) = call(
        joint_kernel, (share, share_other, pay, got, own[0][1]), [rows(64)], COST, unread=1
    )
    got = hub(pay, lambda z, x: (z ^ 1, x), idle_x, "planes_one")
    (far,) = call(far_join_kernel, (pay, got, w_next, w_far), [rows(96)], COST, unread=2)
    (near,) = call(plane_join_kernel, (first, second), [rows(128)], COST)
    other = swap(near, "swap_near")
    acc0, ml0, acc1, ml1 = call(
        plane_kernel,
        (gate, qt, *own[0], *own[1], share_other, first, second, other),
        state * 2,
        COST,
    )
    others = [
        hub(far, lambda z, x, shift=shift: (z, x + shift), idle, "along")
        for shift, idle in ((1, idle_z), (-1, idle_z_odd), (2, idle_z))
    ]
    (far,) = call(row_join_kernel, (far, *others, ml0), [rows(384)], COST, unread=1)
    far_other = swap(far, "swap_far")
    held = ((acc0, ml0), (acc1, ml1))
    halves = []
    for half in range(2):
        after = far_other if half == 0 else halves[0]
        (att,) = call(
            functools.partial(far_kernel, half),
            (gate, qt, *held[half], far, far_other, after),
            [((256, WIDTH), BF16)],
            COST,
            unread=1,
        )
        halves.append(att)
    out = []
    pairs = (PAIR_NEXT, PAIR_FAR)
    for half in range(2):
        peer = lax.ppermute(halves[half], "head", pairs[half])
        keep, send = call(
            functools.partial(project_kernel, half),
            (halves[half], peer, wo, (w_next, w_far)[half]),
            [((256, WIDTH), F32), ((256, WIDTH), BF16)],
            COST,
        )
        out.append(keep + lax.ppermute(send, "head", pairs[1 - half]).astype(F32))
    return jnp.concatenate(out, axis=0).astype(BF16)


def solution(mesh):
    placed = (
        P("seq", None),
        P(None, "head"),
        P(None, "head"),
        P(None, "head"),
        P("head", None),
        P("seq", None),
    )
    return jax.shard_map(
        shards, mesh=mesh, in_specs=placed, out_specs=P("seq", "head"), check_vma=False
    )
```

```python
import functools
import math

import jax
import jax.numpy as jnp
from jax import lax
from jax.experimental import pallas as pl
from jax.experimental.pallas import tpu as pltpu
from jax.sharding import PartitionSpec as P

LOG_TWO = math.log(2.0)
NEG = -1e30
BLOCK = 128
WIDTH = 256
HEADS = 4
F32 = jnp.float32
BF16 = jnp.bfloat16

Z, X, C = 8, 4, 2


def index(z, x, c):
    return (z % Z) * 8 + (x % X) * 2 + c


CHIPS = [(z, x, c) for z in range(Z) for x in range(X) for c in range(C)]


def dot(a, b):
    return lax.dot_general(a, b, (((1,), (0,)), ((), ())), preferred_element_type=F32)


def pool_rows(rows, level):
    token = lax.broadcasted_iota(jnp.int32, (rows, 512), 1)
    row = lax.broadcasted_iota(jnp.int32, (rows, 512), 0)
    inverse = jnp.float32(0.0)
    for each in range(1, 8):
        inverse = jnp.where(level == each, jnp.float32(2.0**-each), inverse)
    hit = lax.shift_right_logical(token, jnp.full((rows, 512), level, jnp.int32)) == row
    return jnp.where(hit, inverse, 0.0).astype(BF16)


def my_core():
    return lax.axis_index("seq") % 2


def load_kernel(
    tok_hbm, wk_hbm, wv_hbm, wo_hbm,
    kv, l1, e1, share, to_next, to_far,
    tok, wk, wv, sems,
):
    head = lax.axis_index("head")
    near, far = next_head(head), 3 - head
    pairs = [(wk_hbm, wk)]
    pairs += [(tok_hbm.at[pl.ds(i * 256, 256)], tok.at[pl.ds(i * 256, 256)]) for i in range(2)]
    pairs.append((wv_hbm, wv))
    for out, first, second in ((to_next, near, 3 - near), (to_far, far, next_head(far))):
        pairs.append((wo_hbm.at[:, columns(first)], out.at[:, pl.ds(0, WIDTH)]))
        pairs.append((wo_hbm.at[:, columns(second)], out.at[:, pl.ds(WIDTH, WIDTH)]))
    copies = [pltpu.make_async_copy(*pair, sems.at[i]) for i, pair in enumerate(pairs)]
    for copy in copies:
        copy.start()
    parts = [
        pool_rows(n, level)
        for n, level in ((128, 1), (64, 3), (32, 4), (128, 2), (16, 5), (16, 6), (16, 7))
    ]
    for copy in copies[:3]:
        copy.wait()
    keys = dot(tok[...], wk[...]).astype(BF16)
    copies[3].wait()
    values = dot(tok[...], wv[...]).astype(BF16)
    both = jnp.concatenate([keys, values], axis=1)
    kv[...] = both
    pooled = dot(jnp.concatenate(parts, axis=0), both)
    l1[...] = pooled[0:128].astype(BF16)
    e1[...] = pooled[128:224].astype(BF16)
    share[...] = pooled[224:400].astype(BF16)
    for copy in copies[4:]:
        copy.wait()


def mirror_kernel(share, other, after, out):
    own, far = share[160:176, :].astype(F32)[:4], other[160:176, :].astype(F32)[:4]
    out[...] = jnp.concatenate([own, far, own, far], axis=0).astype(BF16)


def two_kernel(share, other, got, after0, after1, out):
    own, far = share[144:160, :].astype(F32)[:8], other[144:160, :].astype(F32)[:8]
    out[0:16, :] = jnp.concatenate([own, far], axis=0).astype(BF16)
    out[16:32, :] = got[...]


def joint_kernel(share, other, sent, got, after, out):
    out[0:16, :] = share[128:144, :]
    out[16:32, :] = other[128:144, :]
    out[32:48, :] = got[0:16, :]
    mine, peer = sent[16:32, :].astype(F32)[:8], got[16:32, :].astype(F32)[:8]
    out[48:64, :] = jnp.concatenate([mine, peer], axis=0).astype(BF16)


def far_join_kernel(sent, got, w_next, w_far, out):
    out[0:32, :] = got[0:32, :]
    for level in (1, 2):
        to, at = level * 32, 16 + level * 16
        out[to : to + 16, :] = sent[at : at + 16, :]
        out[to + 16 : to + 32, :] = got[at : at + 16, :]


def near_join_kernel(sent, got, out):
    out[0:32, :] = sent[64:96, :]
    out[32:64, :] = got[64:96, :]


def plane_join_kernel(first, second, out):
    out[0:64, :] = first[0:64, :]
    out[64:128, :] = second[...]


def row_join_kernel(a, b, c, d, after, out):
    for level in range(3):
        for step, piece in enumerate((a, b, c, d)):
            to = level * 128 + step * 32
            out[to : to + 32, :] = piece[level * 32 : (level + 1) * 32, :]


def columns(chunk):
    return pl.ds(pl.multiple_of(chunk * WIDTH, WIDTH), WIDTH)


def next_head(head):
    return head + 1 - 2 * (head % 2)


def stack_heads(query_t):
    head = lax.broadcasted_iota(jnp.int32, (WIDTH, BLOCK), 0) // 64
    zero = jnp.zeros_like(query_t)
    return jnp.concatenate([jnp.where(head == h, query_t, zero) for h in range(HEADS)], axis=1)


def turn(array):
    return array.astype(F32).T.astype(BF16)


def bias_kernel(gate, out):
    seq = lax.axis_index("seq")
    for b in range(4):
        for level in range(8):
            used = gate[b : b + 1, level : level + 1] == 1
            bias = jnp.where(used, jnp.float32(level * LOG_TWO), jnp.float32(NEG))
            if level >= 2:
                bit = lax.shift_right_logical(seq, level - 2) % 2
                bias = jnp.where(bit == 1, bias, jnp.float32(NEG))
            out[b * 8 + level : b * 8 + level + 1, :] = jnp.broadcast_to(bias, (1, BLOCK))


def gate_bias(bias, block, level):
    return bias[block * 8 + level : block * 8 + level + 1, :]


def attend(query_t, keys, values_t, biases, mask, old, old_top, old_total):
    scores = dot(keys, stack_heads(query_t))
    outs, tops, totals = [], [], []
    for h in range(HEADS):
        lanes = slice(h * BLOCK, (h + 1) * BLOCK)
        pieces = [scores[i * BLOCK : (i + 1) * BLOCK, lanes] for i in range(len(biases))]
        if mask is not None:
            pieces[0] = pieces[0] + mask
        top = None if old_top is None else old_top[:, lanes]
        for piece, bias in zip(pieces, biases):
            high = jnp.max(piece, axis=0, keepdims=True) + bias
            top = high if top is None else jnp.maximum(top, high)
        expo = [jnp.exp(piece - (top - bias)) for piece, bias in zip(pieces, biases)]
        total = sum(jnp.sum(piece, axis=0, keepdims=True) for piece in expo)
        weights = jnp.concatenate([piece.astype(BF16) for piece in expo], axis=0)
        rows = slice(h * 64, (h + 1) * 64)
        out = dot(values_t[rows, :], weights)
        if old is not None:
            scale = jnp.exp(old_top[:, lanes] - top)
            out = out + old[rows, :] * scale
            total = total + old_total[:, lanes] * scale
        outs.append(out)
        tops.append(top)
        totals.append(total)
    return outs, tops, totals


def own_half(half, gate, qt, kv, vt, l1, acc, ml):
    key = lax.broadcasted_iota(jnp.int32, (BLOCK, BLOCK), 0)
    row = lax.broadcasted_iota(jnp.int32, (BLOCK, BLOCK), 1)
    causal = jnp.where(key <= row, 0.0, NEG).astype(F32)
    if half:
        l1_t = turn(l1[:, WIDTH:])
    for step in range(2):
        b = half * 2 + step
        rows = slice(b * BLOCK, (b + 1) * BLOCK)
        keys = [kv[rows, :WIDTH]]
        values = [vt[:, rows]]
        biases = [jnp.float32(0.0)]
        if b & 1:
            before = slice((b - 1) * BLOCK, b * BLOCK)
            keys.append(kv[before, :WIDTH])
            values.append(vt[:, before])
            biases.append(gate_bias(gate, b, 0))
        if b & 2:
            keys.append(l1[:, :WIDTH])
            values.append(l1_t)
            biases.append(gate_bias(gate, b, 1))
        keys, values = jnp.concatenate(keys, axis=0), jnp.concatenate(values, axis=1)
        outs, tops, totals = attend(qt[:, rows], keys, values, biases, causal, None, None, None)
        acc[:, step * BLOCK : (step + 1) * BLOCK] = jnp.concatenate(outs, axis=0)
        ml[step : step + 1, :] = jnp.concatenate(tops, axis=1)
        ml[4 + step : 5 + step, :] = jnp.concatenate(totals, axis=1)


def own_blocks(gate, tok, wq, kv, l1, qt, acc0, ml0, acc1, ml1):
    query = dot(tok[...], wq[...]).astype(BF16).astype(F32) * 0.125
    query_t = query.T.astype(BF16)
    qt[...] = query_t
    values_t = turn(kv[:, WIDTH:])
    own_half(0, gate, query_t, kv, values_t, l1, acc0, ml0)
    own_half(1, gate, query_t, kv, values_t, l1, acc1, ml1)


def high_plane():
    return lax.axis_index("seq") >= 32


def early_kernel(gate, tok, wq, kv, l1, *outs):
    @pl.when(jnp.logical_not(high_plane()))
    def _():
        own_blocks(gate, tok, wq, kv, l1, *outs)


def late_kernel(gate, tok, wq, kv, l1, *refs):
    early, outs = refs[:5], refs[-5:]

    @pl.when(high_plane())
    def _():
        own_blocks(gate, tok, wq, kv, l1, *outs)

    @pl.when(jnp.logical_not(high_plane()))
    def _():
        for source, out in zip(early, outs):
            out[...] = source[...]


def level_biases(bias, block, first):
    return [gate_bias(bias, block, level) for level in range(first, first + 3)]


def cross(b, first, gate, qt, acc, ml, keys, values_t):
    step = b % 2
    biases = level_biases(gate, b, first)
    old = (acc[:, step * BLOCK : (step + 1) * BLOCK], ml[step : step + 1, :], ml[4 + step : 5 + step, :])
    return attend(qt[:, b * BLOCK : (b + 1) * BLOCK], keys, values_t, biases, None, *old)


def plane_kernel(gate, qt, acc0, ml0, acc1, ml1, share, first, second, other, *refs):
    outs_refs = refs[-4:]
    pieces = [share[0:128, :], first[0:64, :], other[0:64, :], second[...], other[64:128, :]]
    keys = jnp.concatenate([piece[:, :WIDTH] for piece in pieces], axis=0)
    values_t = turn(jnp.concatenate([piece[:, WIDTH:] for piece in pieces], axis=0))
    for b in range(4):
        half, step = b // 2, b % 2
        acc, ml = ((acc0, ml0), (acc1, ml1))[half]
        acc_out, ml_out = outs_refs[2 * half : 2 * half + 2]
        outs, tops, totals = cross(b, 2, gate, qt, acc, ml, keys, values_t)
        acc_out[:, step * BLOCK : (step + 1) * BLOCK] = jnp.concatenate(outs, axis=0)
        ml_out[step : step + 1, :] = jnp.concatenate(tops, axis=1)
        ml_out[4 + step : 5 + step, :] = jnp.concatenate(totals, axis=1)


def far_kernel(half, gate, qt, acc, ml, mine, other, after, att):
    rows = jnp.where(my_core() == 1, mine[...], other[...])
    keys = rows[:, :WIDTH]
    values_t = turn(rows[:, WIDTH:])
    for step in range(2):
        outs, _, totals = cross(half * 2 + step, 5, gate, qt, acc, ml, keys, values_t)
        outs = [out / total for out, total in zip(outs, totals)]
        turned = jnp.concatenate(outs, axis=0).T.astype(BF16)
        att[step * BLOCK : (step + 1) * BLOCK, :] = turned


def project_kernel(half, mine_att, peer_att, mine_w, peer_w, keep, send):
    head = lax.axis_index("head")
    other = 3 - head if half == 0 else next_head(head)
    for chunk, part, ref in ((other, slice(WIDTH, 2 * WIDTH), send), (head, slice(0, WIDTH), keep)):
        total = dot(mine_att[...], mine_w[:, columns(chunk)]) + dot(peer_att[...], peer_w[:, part])
        ref[...] = total.astype(ref.dtype)


VMEM = pl.BlockSpec(memory_space=pltpu.VMEM)
ANY = pl.BlockSpec(memory_space=pl.ANY)
HBM = pl.BlockSpec(memory_space=pltpu.HBM)


def call(kernel, args, outs, flops, unread=0):
    return pl.pallas_call(
        kernel,
        name=getattr(kernel, "func", kernel).__name__,
        out_shape=[jax.ShapeDtypeStruct(shape, dtype) for shape, dtype in outs],
        in_specs=[VMEM] * (len(args) - unread) + [ANY] * unread,
        out_specs=[VMEM] * len(outs),
        compiler_params=pltpu.CompilerParams(vmem_limit_bytes=24 * 1024 * 1024),
        cost_estimate=pl.CostEstimate(flops=flops, bytes_accessed=1000, transcendentals=0),
    )(*args)


def move(array, pairs, name):
    with jax.named_scope(name):
        return lax.ppermute(array, "seq", pairs)


def hub(array, to, idle, name):
    far = [(index(z, x, 1), index(*to(z, x), 1)) for z, x, c in CHIPS if c]
    near = [(index(z, x, 0), index(*idle(z, x), 0)) for z, x, c in CHIPS if not c]
    return move(array, far + near, name)


def idle_x(z, x):
    return z, x ^ 1


def idle_z(z, x):
    return z ^ 1, x


def across(array, bit, name):
    return move(array, [(index(z, x, c), index(z, x ^ bit, c)) for z, x, c in CHIPS], name)


def swap(array, name):
    return move(array, [(index(z, x, c), index(z, x, 1 - c)) for z, x, c in CHIPS], name)


PAIR_NEXT = [(0, 1), (1, 0), (2, 3), (3, 2)]
PAIR_FAR = [(0, 3), (3, 0), (1, 2), (2, 1)]


COST = 10**6


def shards(tokens, wq, wk, wv, wo, gate):
    rows = lambda n: ((n, 2 * WIDTH), BF16)
    kv, l1, e1, share, to_next, to_far = pl.pallas_call(
        load_kernel,
        name="load_kernel",
        out_shape=[
            jax.ShapeDtypeStruct(shape, BF16)
            for shape in ((512, 512), (128, 512), (96, 512), (176, 512))
            + ((WIDTH, 512),) * 2
        ],
        in_specs=[HBM] * 4,
        out_specs=[VMEM] * 6,
        scratch_shapes=[
            pltpu.VMEM((512, 1024), BF16),
            pltpu.VMEM((1024, WIDTH), BF16),
            pltpu.VMEM((1024, WIDTH), BF16),
            pltpu.SemaphoreType.DMA((8,)),
        ],
        compiler_params=pltpu.CompilerParams(vmem_limit_bytes=105 * 512 * 1024),
        cost_estimate=pl.CostEstimate(flops=COST, bytes_accessed=1000, transcendentals=0),
    )(tokens, wk, wv, wo)
    w_next = lax.ppermute(to_next, "head", PAIR_NEXT)
    w_far = lax.ppermute(to_far, "head", PAIR_FAR)
    share_other = swap(share, "swap_share")
    first = across(e1, 1, "across_one")
    state = [((WIDTH, 256), F32), ((8, 512), F32)]
    held = [((WIDTH, 512), BF16)] + state * 2
    (gate,) = call(bias_kernel, (gate,), [((32, BLOCK), F32)], COST)
    early = call(early_kernel, (gate, tokens, wq, kv, l1), held, COST)
    (pay,) = call(mirror_kernel, (share, share_other, early[2]), [rows(16)], COST, unread=1)
    far5 = hub(pay, lambda z, x: (z ^ 6, x), idle_x, "planes_mirror")
    qt, acc0, ml0, acc1, ml1 = call(
        late_kernel, (gate, tokens, wq, kv, l1, *early, pay), held, COST, unread=1
    )
    own = [(acc0, ml0), (acc1, ml1)]
    first, ml = lax.optimization_barrier((first, own[1][1]))
    own[1] = (own[1][0], ml)
    (near,) = call(near_join_kernel, (e1, first), [rows(64)], COST)
    second = across(near, 2, "across_two")
    (pay,) = call(
        two_kernel, (share, share_other, far5, own[0][1], own[1][1]), [rows(32)], COST, unread=2
    )
    got = hub(pay, lambda z, x: (z ^ 2, x), idle_x, "planes_two")
    (pay,) = call(
        joint_kernel, (share, share_other, pay, got, own[0][1]), [rows(64)], COST, unread=1
    )
    got = hub(pay, lambda z, x: (z ^ 1, x), idle_x, "planes_one")
    (far,) = call(far_join_kernel, (pay, got, w_next, w_far), [rows(96)], COST, unread=2)
    (near,) = call(plane_join_kernel, (first, second), [rows(128)], COST)
    other = swap(near, "swap_near")
    acc0, ml0, acc1, ml1 = call(
        plane_kernel,
        (gate, qt, *own[0], *own[1], share_other, first, second, other),
        state * 2,
        COST,
    )
    others = [hub(far, lambda z, x, shift=shift: (z, x + shift), idle_z, "along") for shift in (1, -1, 2)]
    (far,) = call(row_join_kernel, (far, *others, ml0), [rows(384)], COST, unread=1)
    far_other = swap(far, "swap_far")
    held = ((acc0, ml0), (acc1, ml1))
    halves = []
    for half in range(2):
        after = far_other if half == 0 else halves[0]
        (att,) = call(
            functools.partial(far_kernel, half),
            (gate, qt, *held[half], far, far_other, after),
            [((256, WIDTH), BF16)],
            COST,
            unread=1,
        )
        halves.append(att)
    out = []
    pairs = (PAIR_NEXT, PAIR_FAR)
    for half in range(2):
        peer = lax.ppermute(halves[half], "head", pairs[half])
        keep, send = call(
            functools.partial(project_kernel, half),
            (halves[half], peer, wo, (w_next, w_far)[half]),
            [((256, WIDTH), F32), ((256, WIDTH), BF16)],
            COST,
        )
        out.append(keep + lax.ppermute(send, "head", pairs[1 - half]).astype(F32))
    return jnp.concatenate(out, axis=0).astype(BF16)


def solution(mesh):
    placed = (
        P("seq", None),
        P(None, "head"),
        P(None, "head"),
        P(None, "head"),
        P("head", None),
        P("seq", None),
    )
    return jax.shard_map(
        shards, mesh=mesh, in_specs=placed, out_specs=P("seq", "head"), check_vma=False
    )
```

```python
import functools
import math

import jax
import jax.numpy as jnp
from jax import lax
from jax.experimental import pallas as pl
from jax.experimental.pallas import tpu as pltpu
from jax.sharding import PartitionSpec as P

LOG_TWO = math.log(2.0)
NEG = -1e30
BLOCK = 128
WIDTH = 256
HEADS = 4
F32 = jnp.float32
BF16 = jnp.bfloat16

Z, X, C = 8, 4, 2


def index(z, x, c):
    return (z % Z) * 8 + (x % X) * 2 + c


CHIPS = [(z, x, c) for z in range(Z) for x in range(X) for c in range(C)]


def dot(a, b):
    return lax.dot_general(a, b, (((1,), (0,)), ((), ())), preferred_element_type=F32)


def pool_rows(rows, level):
    token = lax.broadcasted_iota(jnp.int32, (rows, 512), 1)
    row = lax.broadcasted_iota(jnp.int32, (rows, 512), 0)
    inverse = jnp.float32(0.0)
    for each in range(1, 8):
        inverse = jnp.where(level == each, jnp.float32(2.0**-each), inverse)
    hit = lax.shift_right_logical(token, jnp.full((rows, 512), level, jnp.int32)) == row
    return jnp.where(hit, inverse, 0.0).astype(BF16)


def my_core():
    return lax.axis_index("seq") % 2


def load_kernel(
    tok_hbm, wk_hbm, wv_hbm, wo_hbm,
    kv, l1, e1, share, to_next, to_far,
    tok, wk, wv, sems,
):
    head = lax.axis_index("head")
    near, far = next_head(head), 3 - head
    pairs = [(wk_hbm, wk)]
    pairs += [(tok_hbm.at[pl.ds(i * 256, 256)], tok.at[pl.ds(i * 256, 256)]) for i in range(2)]
    pairs.append((wv_hbm, wv))
    for out, first, second in ((to_next, near, 3 - near), (to_far, far, next_head(far))):
        pairs.append((wo_hbm.at[:, columns(first)], out.at[:, pl.ds(0, WIDTH)]))
        pairs.append((wo_hbm.at[:, columns(second)], out.at[:, pl.ds(WIDTH, WIDTH)]))
    copies = [pltpu.make_async_copy(*pair, sems.at[i]) for i, pair in enumerate(pairs)]
    for copy in copies:
        copy.start()
    parts = [
        pool_rows(n, level)
        for n, level in ((128, 1), (64, 3), (32, 4), (128, 2), (16, 5), (16, 6), (16, 7))
    ]
    for copy in copies[:3]:
        copy.wait()
    keys = dot(tok[...], wk[...]).astype(BF16)
    copies[3].wait()
    values = dot(tok[...], wv[...]).astype(BF16)
    both = jnp.concatenate([keys, values], axis=1)
    kv[...] = both
    pooled = dot(jnp.concatenate(parts, axis=0), both)
    l1[...] = pooled[0:128].astype(BF16)
    e1[...] = pooled[128:224].astype(BF16)
    share[...] = pooled[224:400].astype(BF16)
    for copy in copies[4:]:
        copy.wait()


def mirror_kernel(share, other, after, out):
    own, far = share[160:176, :].astype(F32)[:4], other[160:176, :].astype(F32)[:4]
    out[...] = jnp.concatenate([own, far, own, far], axis=0).astype(BF16)


def two_kernel(share, other, got, after0, after1, out):
    own, far = share[144:160, :].astype(F32)[:8], other[144:160, :].astype(F32)[:8]
    out[0:16, :] = jnp.concatenate([own, far], axis=0).astype(BF16)
    out[16:32, :] = got[...]


def joint_kernel(share, other, sent, got, after, out):
    out[0:16, :] = share[128:144, :]
    out[16:32, :] = other[128:144, :]
    out[32:48, :] = got[0:16, :]
    mine, peer = sent[16:32, :].astype(F32)[:8], got[16:32, :].astype(F32)[:8]
    out[48:64, :] = jnp.concatenate([mine, peer], axis=0).astype(BF16)


def far_join_kernel(sent, got, out):
    out[0:32, :] = got[0:32, :]
    for level in (1, 2):
        to, at = level * 32, 16 + level * 16
        out[to : to + 16, :] = sent[at : at + 16, :]
        out[to + 16 : to + 32, :] = got[at : at + 16, :]


def near_join_kernel(sent, got, out):
    out[0:32, :] = sent[64:96, :]
    out[32:64, :] = got[64:96, :]


def plane_join_kernel(first, second, out):
    out[0:64, :] = first[0:64, :]
    out[64:128, :] = second[...]


def row_join_kernel(a, b, c, d, after, out):
    for level in range(3):
        for step, piece in enumerate((a, b, c, d)):
            to = level * 128 + step * 32
            out[to : to + 32, :] = piece[level * 32 : (level + 1) * 32, :]


def columns(chunk):
    return pl.ds(pl.multiple_of(chunk * WIDTH, WIDTH), WIDTH)


def next_head(head):
    return head + 1 - 2 * (head % 2)


def stack_heads(query_t):
    head = lax.broadcasted_iota(jnp.int32, (WIDTH, BLOCK), 0) // 64
    zero = jnp.zeros_like(query_t)
    return jnp.concatenate([jnp.where(head == h, query_t, zero) for h in range(HEADS)], axis=1)


def turn(array):
    return array.astype(F32).T.astype(BF16)


def bias_kernel(gate, out):
    seq = lax.axis_index("seq")
    for b in range(4):
        for level in range(8):
            used = gate[b : b + 1, level : level + 1] == 1
            bias = jnp.where(used, jnp.float32(level * LOG_TWO), jnp.float32(NEG))
            if level >= 2:
                bit = lax.shift_right_logical(seq, level - 2) % 2
                bias = jnp.where(bit == 1, bias, jnp.float32(NEG))
            out[b * 8 + level : b * 8 + level + 1, :] = jnp.broadcast_to(bias, (1, BLOCK))


def gate_bias(bias, block, level):
    return bias[block * 8 + level : block * 8 + level + 1, :]


def attend(query_t, keys, values_t, biases, mask, old, old_top, old_total):
    scores = dot(keys, stack_heads(query_t))
    outs, tops, totals = [], [], []
    for h in range(HEADS):
        lanes = slice(h * BLOCK, (h + 1) * BLOCK)
        pieces = [scores[i * BLOCK : (i + 1) * BLOCK, lanes] for i in range(len(biases))]
        if mask is not None:
            pieces[0] = pieces[0] + mask
        top = None if old_top is None else old_top[:, lanes]
        for piece, bias in zip(pieces, biases):
            high = jnp.max(piece, axis=0, keepdims=True) + bias
            top = high if top is None else jnp.maximum(top, high)
        expo = [jnp.exp(piece - (top - bias)) for piece, bias in zip(pieces, biases)]
        total = sum(jnp.sum(piece, axis=0, keepdims=True) for piece in expo)
        weights = jnp.concatenate([piece.astype(BF16) for piece in expo], axis=0)
        rows = slice(h * 64, (h + 1) * 64)
        out = dot(values_t[rows, :], weights)
        if old is not None:
            scale = jnp.exp(old_top[:, lanes] - top)
            out = out + old[rows, :] * scale
            total = total + old_total[:, lanes] * scale
        outs.append(out)
        tops.append(top)
        totals.append(total)
    return outs, tops, totals


def own_half(half, gate, qt, kv, vt, l1, acc, ml):
    key = lax.broadcasted_iota(jnp.int32, (BLOCK, BLOCK), 0)
    row = lax.broadcasted_iota(jnp.int32, (BLOCK, BLOCK), 1)
    causal = jnp.where(key <= row, 0.0, NEG).astype(F32)
    if half:
        l1_t = turn(l1[:, WIDTH:])
    for step in range(2):
        b = half * 2 + step
        rows = slice(b * BLOCK, (b + 1) * BLOCK)
        keys = [kv[rows, :WIDTH]]
        values = [vt[:, rows]]
        biases = [jnp.float32(0.0)]
        if b & 1:
            before = slice((b - 1) * BLOCK, b * BLOCK)
            keys.append(kv[before, :WIDTH])
            values.append(vt[:, before])
            biases.append(gate_bias(gate, b, 0))
        if b & 2:
            keys.append(l1[:, :WIDTH])
            values.append(l1_t)
            biases.append(gate_bias(gate, b, 1))
        keys, values = jnp.concatenate(keys, axis=0), jnp.concatenate(values, axis=1)
        outs, tops, totals = attend(qt[:, rows], keys, values, biases, causal, None, None, None)
        acc[:, step * BLOCK : (step + 1) * BLOCK] = jnp.concatenate(outs, axis=0)
        ml[step : step + 1, :] = jnp.concatenate(tops, axis=1)
        ml[4 + step : 5 + step, :] = jnp.concatenate(totals, axis=1)


def own_blocks(gate, tok, wq, kv, l1, qt, acc0, ml0, acc1, ml1):
    query = dot(tok[...], wq[...]).astype(BF16).astype(F32) * 0.125
    query_t = query.T.astype(BF16)
    qt[...] = query_t
    values_t = turn(kv[:, WIDTH:])
    own_half(0, gate, query_t, kv, values_t, l1, acc0, ml0)
    own_half(1, gate, query_t, kv, values_t, l1, acc1, ml1)


def high_plane():
    return lax.axis_index("seq") >= 32


def early_kernel(gate, tok, wq, kv, l1, *outs):
    @pl.when(jnp.logical_not(high_plane()))
    def _():
        own_blocks(gate, tok, wq, kv, l1, *outs)


def late_kernel(gate, tok, wq, kv, l1, *refs):
    early, outs = refs[:5], refs[-5:]

    @pl.when(high_plane())
    def _():
        own_blocks(gate, tok, wq, kv, l1, *outs)

    @pl.when(jnp.logical_not(high_plane()))
    def _():
        for source, out in zip(early, outs):
            out[...] = source[...]


def level_biases(bias, block, first):
    return [gate_bias(bias, block, level) for level in range(first, first + 3)]


def cross(b, first, gate, qt, acc, ml, keys, values_t):
    step = b % 2
    biases = level_biases(gate, b, first)
    old = (acc[:, step * BLOCK : (step + 1) * BLOCK], ml[step : step + 1, :], ml[4 + step : 5 + step, :])
    return attend(qt[:, b * BLOCK : (b + 1) * BLOCK], keys, values_t, biases, None, *old)


def plane_kernel(gate, qt, acc0, ml0, acc1, ml1, share, first, second, other, *refs):
    outs_refs = refs[-4:]
    pieces = [share[0:128, :], first[0:64, :], other[0:64, :], second[...], other[64:128, :]]
    keys = jnp.concatenate([piece[:, :WIDTH] for piece in pieces], axis=0)
    values_t = turn(jnp.concatenate([piece[:, WIDTH:] for piece in pieces], axis=0))
    for b in range(4):
        half, step = b // 2, b % 2
        acc, ml = ((acc0, ml0), (acc1, ml1))[half]
        acc_out, ml_out = outs_refs[2 * half : 2 * half + 2]
        outs, tops, totals = cross(b, 2, gate, qt, acc, ml, keys, values_t)
        acc_out[:, step * BLOCK : (step + 1) * BLOCK] = jnp.concatenate(outs, axis=0)
        ml_out[step : step + 1, :] = jnp.concatenate(tops, axis=1)
        ml_out[4 + step : 5 + step, :] = jnp.concatenate(totals, axis=1)


def far_kernel(half, gate, qt, acc, ml, mine, other, after, att):
    rows = jnp.where(my_core() == 1, mine[...], other[...])
    keys = rows[:, :WIDTH]
    values_t = turn(rows[:, WIDTH:])
    for step in range(2):
        outs, _, totals = cross(half * 2 + step, 5, gate, qt, acc, ml, keys, values_t)
        outs = [out / total for out, total in zip(outs, totals)]
        turned = jnp.concatenate(outs, axis=0).T.astype(BF16)
        att[step * BLOCK : (step + 1) * BLOCK, :] = turned


def project_kernel(half, mine_att, peer_att, mine_w, peer_w, keep, send):
    head = lax.axis_index("head")
    other = 3 - head if half == 0 else next_head(head)
    for chunk, part, ref in ((other, slice(WIDTH, 2 * WIDTH), send), (head, slice(0, WIDTH), keep)):
        total = dot(mine_att[...], mine_w[:, columns(chunk)]) + dot(peer_att[...], peer_w[:, part])
        ref[...] = total.astype(ref.dtype)


VMEM = pl.BlockSpec(memory_space=pltpu.VMEM)
ANY = pl.BlockSpec(memory_space=pl.ANY)
HBM = pl.BlockSpec(memory_space=pltpu.HBM)


def call(kernel, args, outs, flops, unread=0):
    return pl.pallas_call(
        kernel,
        name=getattr(kernel, "func", kernel).__name__,
        out_shape=[jax.ShapeDtypeStruct(shape, dtype) for shape, dtype in outs],
        in_specs=[VMEM] * (len(args) - unread) + [ANY] * unread,
        out_specs=[VMEM] * len(outs),
        compiler_params=pltpu.CompilerParams(vmem_limit_bytes=24 * 1024 * 1024),
        cost_estimate=pl.CostEstimate(flops=flops, bytes_accessed=1000, transcendentals=0),
    )(*args)


def move(array, pairs, name):
    with jax.named_scope(name):
        return lax.ppermute(array, "seq", pairs)


def hub(array, to, idle, name):
    far = [(index(z, x, 1), index(*to(z, x), 1)) for z, x, c in CHIPS if c]
    near = [(index(z, x, 0), index(*idle(z, x), 0)) for z, x, c in CHIPS if not c]
    return move(array, far + near, name)


def idle_x(z, x):
    return z, x ^ 1


def idle_z(z, x):
    return z ^ 1, x


def across(array, bit, name):
    return move(array, [(index(z, x, c), index(z, x ^ bit, c)) for z, x, c in CHIPS], name)


def swap(array, name):
    return move(array, [(index(z, x, c), index(z, x, 1 - c)) for z, x, c in CHIPS], name)


PAIR_NEXT = [(0, 1), (1, 0), (2, 3), (3, 2)]
PAIR_FAR = [(0, 3), (3, 0), (1, 2), (2, 1)]


COST = 10**6


def shards(tokens, wq, wk, wv, wo, gate):
    rows = lambda n: ((n, 2 * WIDTH), BF16)
    kv, l1, e1, share, to_next, to_far = pl.pallas_call(
        load_kernel,
        name="load_kernel",
        out_shape=[
            jax.ShapeDtypeStruct(shape, BF16)
            for shape in ((512, 512), (128, 512), (96, 512), (176, 512))
            + ((WIDTH, 512),) * 2
        ],
        in_specs=[HBM] * 4,
        out_specs=[VMEM] * 6,
        scratch_shapes=[
            pltpu.VMEM((512, 1024), BF16),
            pltpu.VMEM((1024, WIDTH), BF16),
            pltpu.VMEM((1024, WIDTH), BF16),
            pltpu.SemaphoreType.DMA((8,)),
        ],
        compiler_params=pltpu.CompilerParams(vmem_limit_bytes=105 * 512 * 1024),
        cost_estimate=pl.CostEstimate(flops=COST, bytes_accessed=1000, transcendentals=0),
    )(tokens, wk, wv, wo)
    share_other = swap(share, "swap_share")
    first = across(e1, 1, "across_one")
    state = [((WIDTH, 256), F32), ((8, 512), F32)]
    held = [((WIDTH, 512), BF16)] + state * 2
    (gate,) = call(bias_kernel, (gate,), [((32, BLOCK), F32)], COST)
    early = call(early_kernel, (gate, tokens, wq, kv, l1), held, COST)
    (pay,) = call(mirror_kernel, (share, share_other, early[2]), [rows(16)], COST, unread=1)
    far5 = hub(pay, lambda z, x: (z ^ 6, x), idle_x, "planes_mirror")
    qt, acc0, ml0, acc1, ml1 = call(
        late_kernel, (gate, tokens, wq, kv, l1, *early, pay), held, COST, unread=1
    )
    own = [(acc0, ml0), (acc1, ml1)]
    first, ml = lax.optimization_barrier((first, own[1][1]))
    own[1] = (own[1][0], ml)
    (near,) = call(near_join_kernel, (e1, first), [rows(64)], COST)
    second = across(near, 2, "across_two")
    (pay,) = call(
        two_kernel, (share, share_other, far5, own[0][1], own[1][1]), [rows(32)], COST, unread=2
    )
    got = hub(pay, lambda z, x: (z ^ 2, x), idle_x, "planes_two")
    (pay,) = call(
        joint_kernel, (share, share_other, pay, got, own[0][1]), [rows(64)], COST, unread=1
    )
    got = hub(pay, lambda z, x: (z ^ 1, x), idle_x, "planes_one")
    (far,) = call(far_join_kernel, (pay, got), [rows(96)], COST)
    (near,) = call(plane_join_kernel, (first, second), [rows(128)], COST)
    other = swap(near, "swap_near")
    far, to_far, to_next = lax.optimization_barrier((far, to_far, to_next))
    w_next = lax.ppermute(to_next, "head", PAIR_NEXT)
    w_far = lax.ppermute(to_far, "head", PAIR_FAR)
    acc0, ml0, acc1, ml1 = call(
        plane_kernel,
        (gate, qt, *own[0], *own[1], share_other, first, second, other),
        state * 2,
        COST,
    )
    others = [hub(far, lambda z, x, shift=shift: (z, x + shift), idle_z, "along") for shift in (1, -1, 2)]
    (far,) = call(row_join_kernel, (far, *others, ml0), [rows(384)], COST, unread=1)
    far_other = swap(far, "swap_far")
    held = ((acc0, ml0), (acc1, ml1))
    halves = []
    for half in range(2):
        after = far_other if half == 0 else halves[0]
        (att,) = call(
            functools.partial(far_kernel, half),
            (gate, qt, *held[half], far, far_other, after),
            [((256, WIDTH), BF16)],
            COST,
            unread=1,
        )
        halves.append(att)
    out = []
    pairs = (PAIR_NEXT, PAIR_FAR)
    for half in range(2):
        peer = lax.ppermute(halves[half], "head", pairs[half])
        keep, send = call(
            functools.partial(project_kernel, half),
            (halves[half], peer, wo, (w_next, w_far)[half]),
            [((256, WIDTH), F32), ((256, WIDTH), BF16)],
            COST,
        )
        out.append(keep + lax.ppermute(send, "head", pairs[1 - half]).astype(F32))
    return jnp.concatenate(out, axis=0).astype(BF16)


def solution(mesh):
    placed = (
        P("seq", None),
        P(None, "head"),
        P(None, "head"),
        P(None, "head"),
        P("head", None),
        P("seq", None),
    )
    return jax.shard_map(
        shards, mesh=mesh, in_specs=placed, out_specs=P("seq", "head"), check_vma=False
    )
```

```python
import functools
import math

import jax
import jax.numpy as jnp
from jax import lax
from jax.experimental import pallas as pl
from jax.experimental.pallas import tpu as pltpu
from jax.sharding import PartitionSpec as P

LOG_TWO = math.log(2.0)
NEG = -1e30
BLOCK = 128
WIDTH = 256
HEADS = 4
F32 = jnp.float32
BF16 = jnp.bfloat16

Z, X, C = 8, 4, 2


def index(z, x, c):
    return (z % Z) * 8 + (x % X) * 2 + c


CHIPS = [(z, x, c) for z in range(Z) for x in range(X) for c in range(C)]


def dot(a, b):
    return lax.dot_general(a, b, (((1,), (0,)), ((), ())), preferred_element_type=F32)


def pool_rows(rows, level):
    token = lax.broadcasted_iota(jnp.int32, (rows, 512), 1)
    row = lax.broadcasted_iota(jnp.int32, (rows, 512), 0)
    inverse = jnp.float32(0.0)
    for each in range(1, 8):
        inverse = jnp.where(level == each, jnp.float32(2.0**-each), inverse)
    hit = lax.shift_right_logical(token, jnp.full((rows, 512), level, jnp.int32)) == row
    return jnp.where(hit, inverse, 0.0).astype(BF16)


def my_core():
    return lax.axis_index("seq") % 2


def load_kernel(
    tok_hbm, wk_hbm, wv_hbm, wo_hbm,
    kv, l1, e1, share, to_next, to_far,
    tok, wk, wv, sems,
):
    head = lax.axis_index("head")
    near, far = next_head(head), 3 - head
    pairs = [(wk_hbm, wk)]
    pairs += [(tok_hbm.at[pl.ds(i * 256, 256)], tok.at[pl.ds(i * 256, 256)]) for i in range(2)]
    pairs.append((wv_hbm, wv))
    for out, first, second in ((to_next, near, 3 - near), (to_far, far, next_head(far))):
        pairs.append((wo_hbm.at[:, columns(first)], out.at[:, pl.ds(0, WIDTH)]))
        pairs.append((wo_hbm.at[:, columns(second)], out.at[:, pl.ds(WIDTH, WIDTH)]))
    copies = [pltpu.make_async_copy(*pair, sems.at[i]) for i, pair in enumerate(pairs)]
    for copy in copies:
        copy.start()
    parts = [
        pool_rows(n, level)
        for n, level in ((128, 1), (64, 3), (32, 4), (128, 2), (16, 5), (16, 6), (16, 7))
    ]
    for copy in copies[:3]:
        copy.wait()
    keys = dot(tok[...], wk[...]).astype(BF16)
    copies[3].wait()
    values = dot(tok[...], wv[...]).astype(BF16)
    both = jnp.concatenate([keys, values], axis=1)
    kv[...] = both
    pooled = dot(jnp.concatenate(parts, axis=0), both)
    l1[...] = pooled[0:128].astype(BF16)
    e1[...] = pooled[128:224].astype(BF16)
    share[...] = pooled[224:400].astype(BF16)
    for copy in copies[4:]:
        copy.wait()


def mirror_kernel(share, other, after, out):
    own, far = share[160:176, :].astype(F32)[:4], other[160:176, :].astype(F32)[:4]
    out[...] = jnp.concatenate([own, far, own, far], axis=0).astype(BF16)


def two_kernel(share, other, got, after0, after1, out):
    own, far = share[144:160, :].astype(F32)[:8], other[144:160, :].astype(F32)[:8]
    out[0:16, :] = jnp.concatenate([own, far], axis=0).astype(BF16)
    out[16:32, :] = got[...]


def joint_kernel(share, other, sent, got, after, out):
    out[0:16, :] = share[128:144, :]
    out[16:32, :] = other[128:144, :]
    out[32:48, :] = got[0:16, :]
    mine, peer = sent[16:32, :].astype(F32)[:8], got[16:32, :].astype(F32)[:8]
    out[48:64, :] = jnp.concatenate([mine, peer], axis=0).astype(BF16)


def far_join_kernel(sent, got, w_next, out):
    out[0:32, :] = got[0:32, :]
    for level in (1, 2):
        to, at = level * 32, 16 + level * 16
        out[to : to + 16, :] = sent[at : at + 16, :]
        out[to + 16 : to + 32, :] = got[at : at + 16, :]


def near_join_kernel(sent, got, out):
    out[0:32, :] = sent[64:96, :]
    out[32:64, :] = got[64:96, :]


def plane_join_kernel(first, second, out):
    out[0:64, :] = first[0:64, :]
    out[64:128, :] = second[...]


def row_join_kernel(a, b, c, d, after, out):
    for level in range(3):
        for step, piece in enumerate((a, b, c, d)):
            to = level * 128 + step * 32
            out[to : to + 32, :] = piece[level * 32 : (level + 1) * 32, :]


def columns(chunk):
    return pl.ds(pl.multiple_of(chunk * WIDTH, WIDTH), WIDTH)


def next_head(head):
    return head + 1 - 2 * (head % 2)


def stack_heads(query_t):
    head = lax.broadcasted_iota(jnp.int32, (WIDTH, BLOCK), 0) // 64
    zero = jnp.zeros_like(query_t)
    return jnp.concatenate([jnp.where(head == h, query_t, zero) for h in range(HEADS)], axis=1)


def turn(array):
    return array.astype(F32).T.astype(BF16)


def bias_kernel(gate, out):
    seq = lax.axis_index("seq")
    for b in range(4):
        for level in range(8):
            used = gate[b : b + 1, level : level + 1] == 1
            bias = jnp.where(used, jnp.float32(level * LOG_TWO), jnp.float32(NEG))
            if level >= 2:
                bit = lax.shift_right_logical(seq, level - 2) % 2
                bias = jnp.where(bit == 1, bias, jnp.float32(NEG))
            out[b * 8 + level : b * 8 + level + 1, :] = jnp.broadcast_to(bias, (1, BLOCK))


def gate_bias(bias, block, level):
    return bias[block * 8 + level : block * 8 + level + 1, :]


def attend(query_t, keys, values_t, biases, mask, old, old_top, old_total):
    scores = dot(keys, stack_heads(query_t))
    outs, tops, totals = [], [], []
    for h in range(HEADS):
        lanes = slice(h * BLOCK, (h + 1) * BLOCK)
        pieces = [scores[i * BLOCK : (i + 1) * BLOCK, lanes] for i in range(len(biases))]
        if mask is not None:
            pieces[0] = pieces[0] + mask
        top = None if old_top is None else old_top[:, lanes]
        for piece, bias in zip(pieces, biases):
            high = jnp.max(piece, axis=0, keepdims=True) + bias
            top = high if top is None else jnp.maximum(top, high)
        expo = [jnp.exp(piece - (top - bias)) for piece, bias in zip(pieces, biases)]
        total = sum(jnp.sum(piece, axis=0, keepdims=True) for piece in expo)
        weights = jnp.concatenate([piece.astype(BF16) for piece in expo], axis=0)
        rows = slice(h * 64, (h + 1) * 64)
        out = dot(values_t[rows, :], weights)
        if old is not None:
            scale = jnp.exp(old_top[:, lanes] - top)
            out = out + old[rows, :] * scale
            total = total + old_total[:, lanes] * scale
        outs.append(out)
        tops.append(top)
        totals.append(total)
    return outs, tops, totals


def own_half(half, gate, qt, kv, vt, l1, acc, ml):
    key = lax.broadcasted_iota(jnp.int32, (BLOCK, BLOCK), 0)
    row = lax.broadcasted_iota(jnp.int32, (BLOCK, BLOCK), 1)
    causal = jnp.where(key <= row, 0.0, NEG).astype(F32)
    if half:
        l1_t = turn(l1[:, WIDTH:])
    for step in range(2):
        b = half * 2 + step
        rows = slice(b * BLOCK, (b + 1) * BLOCK)
        keys = [kv[rows, :WIDTH]]
        values = [vt[:, rows]]
        biases = [jnp.float32(0.0)]
        if b & 1:
            before = slice((b - 1) * BLOCK, b * BLOCK)
            keys.append(kv[before, :WIDTH])
            values.append(vt[:, before])
            biases.append(gate_bias(gate, b, 0))
        if b & 2:
            keys.append(l1[:, :WIDTH])
            values.append(l1_t)
            biases.append(gate_bias(gate, b, 1))
        keys, values = jnp.concatenate(keys, axis=0), jnp.concatenate(values, axis=1)
        outs, tops, totals = attend(qt[:, rows], keys, values, biases, causal, None, None, None)
        acc[:, step * BLOCK : (step + 1) * BLOCK] = jnp.concatenate(outs, axis=0)
        ml[step : step + 1, :] = jnp.concatenate(tops, axis=1)
        ml[4 + step : 5 + step, :] = jnp.concatenate(totals, axis=1)


def own_blocks(gate, tok, wq, kv, l1, qt, acc0, ml0, acc1, ml1):
    query = dot(tok[...], wq[...]).astype(BF16).astype(F32) * 0.125
    query_t = query.T.astype(BF16)
    qt[...] = query_t
    values_t = turn(kv[:, WIDTH:])
    own_half(0, gate, query_t, kv, values_t, l1, acc0, ml0)
    own_half(1, gate, query_t, kv, values_t, l1, acc1, ml1)


def high_plane():
    return lax.axis_index("seq") >= 32


def early_kernel(gate, tok, wq, kv, l1, *outs):
    @pl.when(jnp.logical_not(high_plane()))
    def _():
        own_blocks(gate, tok, wq, kv, l1, *outs)


def late_kernel(gate, tok, wq, kv, l1, *refs):
    early, outs = refs[:5], refs[-5:]

    @pl.when(high_plane())
    def _():
        own_blocks(gate, tok, wq, kv, l1, *outs)

    @pl.when(jnp.logical_not(high_plane()))
    def _():
        for source, out in zip(early, outs):
            out[...] = source[...]


def level_biases(bias, block, first):
    return [gate_bias(bias, block, level) for level in range(first, first + 3)]


def cross(b, first, gate, qt, acc, ml, keys, values_t):
    step = b % 2
    biases = level_biases(gate, b, first)
    old = (acc[:, step * BLOCK : (step + 1) * BLOCK], ml[step : step + 1, :], ml[4 + step : 5 + step, :])
    return attend(qt[:, b * BLOCK : (b + 1) * BLOCK], keys, values_t, biases, None, *old)


def plane_kernel(gate, qt, acc0, ml0, acc1, ml1, share, first, second, other, *refs):
    outs_refs = refs[-4:]
    pieces = [share[0:128, :], first[0:64, :], other[0:64, :], second[...], other[64:128, :]]
    keys = jnp.concatenate([piece[:, :WIDTH] for piece in pieces], axis=0)
    values_t = turn(jnp.concatenate([piece[:, WIDTH:] for piece in pieces], axis=0))
    for b in range(4):
        half, step = b // 2, b % 2
        acc, ml = ((acc0, ml0), (acc1, ml1))[half]
        acc_out, ml_out = outs_refs[2 * half : 2 * half + 2]
        outs, tops, totals = cross(b, 2, gate, qt, acc, ml, keys, values_t)
        acc_out[:, step * BLOCK : (step + 1) * BLOCK] = jnp.concatenate(outs, axis=0)
        ml_out[step : step + 1, :] = jnp.concatenate(tops, axis=1)
        ml_out[4 + step : 5 + step, :] = jnp.concatenate(totals, axis=1)


def far_kernel(half, gate, qt, acc, ml, mine, other, after, att):
    rows = jnp.where(my_core() == 1, mine[...], other[...])
    keys = rows[:, :WIDTH]
    values_t = turn(rows[:, WIDTH:])
    for step in range(2):
        outs, _, totals = cross(half * 2 + step, 5, gate, qt, acc, ml, keys, values_t)
        outs = [out / total for out, total in zip(outs, totals)]
        turned = jnp.concatenate(outs, axis=0).T.astype(BF16)
        att[step * BLOCK : (step + 1) * BLOCK, :] = turned


def project_kernel(half, mine_att, peer_att, mine_w, peer_w, keep, send):
    head = lax.axis_index("head")
    other = 3 - head if half == 0 else next_head(head)
    for chunk, part, ref in ((other, slice(WIDTH, 2 * WIDTH), send), (head, slice(0, WIDTH), keep)):
        total = dot(mine_att[...], mine_w[:, columns(chunk)]) + dot(peer_att[...], peer_w[:, part])
        ref[...] = total.astype(ref.dtype)


VMEM = pl.BlockSpec(memory_space=pltpu.VMEM)
ANY = pl.BlockSpec(memory_space=pl.ANY)
HBM = pl.BlockSpec(memory_space=pltpu.HBM)


def call(kernel, args, outs, flops, unread=0):
    return pl.pallas_call(
        kernel,
        name=getattr(kernel, "func", kernel).__name__,
        out_shape=[jax.ShapeDtypeStruct(shape, dtype) for shape, dtype in outs],
        in_specs=[VMEM] * (len(args) - unread) + [ANY] * unread,
        out_specs=[VMEM] * len(outs),
        compiler_params=pltpu.CompilerParams(vmem_limit_bytes=24 * 1024 * 1024),
        cost_estimate=pl.CostEstimate(flops=flops, bytes_accessed=1000, transcendentals=0),
    )(*args)


def move(array, pairs, name):
    with jax.named_scope(name):
        return lax.ppermute(array, "seq", pairs)


def hub(array, to, idle, name):
    far = [(index(z, x, 1), index(*to(z, x), 1)) for z, x, c in CHIPS if c]
    near = [(index(z, x, 0), index(*idle(z, x), 0)) for z, x, c in CHIPS if not c]
    return move(array, far + near, name)


def idle_x(z, x):
    return z, x ^ 1


def idle_z(z, x):
    return z ^ 1, x


def across(array, bit, name):
    return move(array, [(index(z, x, c), index(z, x ^ bit, c)) for z, x, c in CHIPS], name)


def swap(array, name):
    return move(array, [(index(z, x, c), index(z, x, 1 - c)) for z, x, c in CHIPS], name)


PAIR_NEXT = [(0, 1), (1, 0), (2, 3), (3, 2)]
PAIR_FAR = [(0, 3), (3, 0), (1, 2), (2, 1)]


COST = 10**6


def shards(tokens, wq, wk, wv, wo, gate):
    rows = lambda n: ((n, 2 * WIDTH), BF16)
    kv, l1, e1, share, to_next, to_far = pl.pallas_call(
        load_kernel,
        name="load_kernel",
        out_shape=[
            jax.ShapeDtypeStruct(shape, BF16)
            for shape in ((512, 512), (128, 512), (96, 512), (176, 512))
            + ((WIDTH, 512),) * 2
        ],
        in_specs=[HBM] * 4,
        out_specs=[VMEM] * 6,
        scratch_shapes=[
            pltpu.VMEM((512, 1024), BF16),
            pltpu.VMEM((1024, WIDTH), BF16),
            pltpu.VMEM((1024, WIDTH), BF16),
            pltpu.SemaphoreType.DMA((8,)),
        ],
        compiler_params=pltpu.CompilerParams(vmem_limit_bytes=105 * 512 * 1024),
        cost_estimate=pl.CostEstimate(flops=COST, bytes_accessed=1000, transcendentals=0),
    )(tokens, wk, wv, wo)
    w_next = lax.ppermute(to_next, "head", PAIR_NEXT)
    share_other = swap(share, "swap_share")
    first = across(e1, 1, "across_one")
    state = [((WIDTH, 256), F32), ((8, 512), F32)]
    held = [((WIDTH, 512), BF16)] + state * 2
    (gate,) = call(bias_kernel, (gate,), [((32, BLOCK), F32)], COST)
    early = call(early_kernel, (gate, tokens, wq, kv, l1), held, COST)
    (pay,) = call(mirror_kernel, (share, share_other, early[2]), [rows(16)], COST, unread=1)
    far5 = hub(pay, lambda z, x: (z ^ 6, x), idle_x, "planes_mirror")
    qt, acc0, ml0, acc1, ml1 = call(
        late_kernel, (gate, tokens, wq, kv, l1, *early, pay), held, COST, unread=1
    )
    own = [(acc0, ml0), (acc1, ml1)]
    first, ml = lax.optimization_barrier((first, own[1][1]))
    own[1] = (own[1][0], ml)
    (near,) = call(near_join_kernel, (e1, first), [rows(64)], COST)
    second = across(near, 2, "across_two")
    (pay,) = call(
        two_kernel, (share, share_other, far5, own[0][1], own[1][1]), [rows(32)], COST, unread=2
    )
    got = hub(pay, lambda z, x: (z ^ 2, x), idle_x, "planes_two")
    (pay,) = call(
        joint_kernel, (share, share_other, pay, got, own[0][1]), [rows(64)], COST, unread=1
    )
    got = hub(pay, lambda z, x: (z ^ 1, x), idle_x, "planes_one")
    (far,) = call(far_join_kernel, (pay, got, w_next), [rows(96)], COST, unread=1)
    (near,) = call(plane_join_kernel, (first, second), [rows(128)], COST)
    other = swap(near, "swap_near")
    far, to_far = lax.optimization_barrier((far, to_far))
    w_far = lax.ppermute(to_far, "head", PAIR_FAR)
    acc0, ml0, acc1, ml1 = call(
        plane_kernel,
        (gate, qt, *own[0], *own[1], share_other, first, second, other),
        state * 2,
        COST,
    )
    others = [hub(far, lambda z, x, shift=shift: (z, x + shift), idle_z, "along") for shift in (1, -1, 2)]
    (far,) = call(row_join_kernel, (far, *others, ml0), [rows(384)], COST, unread=1)
    far_other = swap(far, "swap_far")
    held = ((acc0, ml0), (acc1, ml1))
    halves = []
    for half in range(2):
        after = far_other if half == 0 else halves[0]
        (att,) = call(
            functools.partial(far_kernel, half),
            (gate, qt, *held[half], far, far_other, after),
            [((256, WIDTH), BF16)],
            COST,
            unread=1,
        )
        halves.append(att)
    out = []
    pairs = (PAIR_NEXT, PAIR_FAR)
    for half in range(2):
        peer = lax.ppermute(halves[half], "head", pairs[half])
        keep, send = call(
            functools.partial(project_kernel, half),
            (halves[half], peer, wo, (w_next, w_far)[half]),
            [((256, WIDTH), F32), ((256, WIDTH), BF16)],
            COST,
        )
        out.append(keep + lax.ppermute(send, "head", pairs[1 - half]).astype(F32))
    return jnp.concatenate(out, axis=0).astype(BF16)


def solution(mesh):
    placed = (
        P("seq", None),
        P(None, "head"),
        P(None, "head"),
        P(None, "head"),
        P("head", None),
        P("seq", None),
    )
    return jax.shard_map(
        shards, mesh=mesh, in_specs=placed, out_specs=P("seq", "head"), check_vma=False
    )
```
